512 devices in a mesh: grid: 64 (over x, y_lo, z), member: 8 (over y_hi, core).
Axes of the slice: x: 4, y: 8 (y_hi: 4, y_lo: 2; y = y_hi * 2 + y_lo), z: 8, core: 2. Of those that a mesh axis runs over, the one named last changes fastest.
Arguments:
- fields: bfloat16 [8, 65536, 1024], P('member', 'grid'), may hold values from -0.796875 to 0.796875
- observed: bfloat16 [100, 65536], P(None, 'grid'), may hold values from -6 to 6
- lat_weight: float32 [65536], P('grid'), may hold values from 0.3 to 6, as said below
- var_weight: float32 [100], replicated, may hold values from 0.25 to 4
- weight: bfloat16 [100, 1024], replicated, may hold values from -0.1875 to 0.1875
- bias: float32 [100], replicated, may hold values from -1 to 1
- gain: float32 [1024], replicated, may hold values from 0.1 to 1.9
Outputs:
- grad_fields: bfloat16 [8, 65536, 1024], P('member', 'grid')
- grad_weight: float32 [100, 1024], replicated
- grad_gain: float32 [1024], replicated
- grad_bias: float32 [100], replicated
- loss: float32 [], replicated
The draws below stay inside these ranges and needn't reach their ends.
Inputs may be any that keep to these rules, and one draw needn't show every extreme that they name: `lat_weight`: positive.
All inputs are finite; a program needn't handle non-finite values.
Results may differ from the reference program's by a relative error of at most 0.0014.
The reference program's roundings to bfloat16 on the way (of `normed` and `grad_pred`) count: a program that leaves them out, or rounds other values in their place, can miss the bound.
Values sent between devices are 32-bit elements; how exact they have to be, the bound alone decides.
No kernel may reach another device: no remote copies, remote signals or barrier semaphores. Data moves between devices by JAX's collectives and lax.ppermute only.
A program may use at most 64 MiB of HBM per device.

```python
import math
import jax
import jax.numpy as jnp
from jax import lax

D = 1024
VARS = 100
MEMBERS = 8
POINTS = 65536


def draw_lat_weight(key, part):
    inner = jax.random.fold_in(key, 17)
    places = jnp.arange(POINTS).astype(jnp.float32)
    profile = 1.0 + 3.0 * places / POINTS
    factors = jax.random.uniform(inner, (POINTS,), jnp.float32, 0.5, 1.5)
    return (profile * factors).astype(jnp.float32)


def steps_of(key, shape, shards, smallest, high):
    level, own = 1.0, jax.random.fold_in(key, 6)
    for position, shards_of in shards:
        heights = jnp.exp(jax.random.uniform(jax.random.fold_in(own, position), (shards_of,), jnp.float32, smallest / len(shards), high / len(shards)))
        level = level * jnp.repeat(heights, shape[position] // shards_of).reshape([-1 if axis == position else 1 for axis in range(len(shape))])
    return level


def bell_draw(key, extent, width, most, pieces=(), kind=jnp.bfloat16):
    factor_of = steps_of(key, extent, pieces, -0.22, 0.18) if pieces else 1.0
    entries = jax.random.normal(key, extent, jnp.float32) * width * factor_of
    return jnp.minimum(jnp.maximum(entries, -most), most).astype(kind)


def setup_inputs(seed: int = 0) -> dict:
    streams_of = jax.random.split(jax.random.key(seed), 8)
    fields = bell_draw(streams_of[0], (MEMBERS, POINTS, D), 0.1, 0.796875, ((0, 8), (1, 64)))
    observed = bell_draw(streams_of[1], (VARS, POINTS), 1.0, 6.0, ((1, 64),))
    lat_weight = draw_lat_weight(jax.random.fold_in(streams_of[7], 71), 0)
    var_weight = jnp.clip(jnp.exp(jax.random.uniform(streams_of[3], (VARS,), jnp.float32, math.log(0.25), math.log(4.0))), 0.25, 4.0)
    weight = bell_draw(streams_of[4], (VARS, D), D ** -0.5, 0.1875)
    bias = jnp.clip(jax.random.uniform(streams_of[5], (VARS,), jnp.float32, -1.0, 1.0), -1.0, 1.0)
    gain = jnp.clip(1.0 + 0.18 * jax.random.normal(streams_of[6], (D,), jnp.float32), 0.1, 1.9)
    return dict(fields=fields, observed=observed, lat_weight=lat_weight, var_weight=var_weight, weight=weight, bias=bias, gain=gain)


soft_square = 0.01
norm_epsilon = 1e-05

def normalize(member_rows, gain):
    values = member_rows.astype(jnp.float32)
    row_mean = lax.optimization_barrier(jnp.mean(values, axis=-1, keepdims=True))
    centred = values - row_mean
    inv_std = lax.rsqrt(lax.optimization_barrier(jnp.mean(centred * centred, axis=-1, keepdims=True)) + norm_epsilon)
    unit_rows = centred * inv_std
    normed = (unit_rows * gain[None, :]).astype(jnp.bfloat16)
    return (normed, unit_rows, inv_std)

def reference(fields, observed, lat_weight, var_weight, weight, bias, gain):
    members = fields.shape[0]

    def forward(member_rows):
        normed, unit_rows, inv_std = normalize(member_rows, gain)
        return jnp.dot(weight, normed.T, preferred_element_type=jnp.float32) + bias[:, None]
    predicted = lax.map(forward, fields)
    target = observed.astype(jnp.float32)
    obs_gap = predicted - target[None]
    obs_abs = jnp.sqrt(obs_gap * obs_gap + soft_square)
    obs_sign = obs_gap / obs_abs
    sign_rows = [jnp.zeros(target.shape, jnp.float32) for member in range(members)]
    pair_abs = jnp.zeros(target.shape, jnp.float32)
    for first in range(members):
        for second in range(first + 1, members):
            gap = predicted[first] - predicted[second]
            soft_abs = jnp.sqrt(gap * gap + soft_square)
            pair_abs = pair_abs + soft_abs
            sign_rows[first] = sign_rows[first] + gap / soft_abs
            sign_rows[second] = sign_rows[second] - gap / soft_abs
    pair_sign = jnp.stack(sign_rows)
    scale_pair = 1.0 / (members * (members - 1))
    weight_grid = var_weight[:, None] * lat_weight[None, :]
    crps = lax.optimization_barrier(jnp.sum(obs_abs, axis=0)) / members - pair_abs * scale_pair
    lat_total = jnp.sum(lat_weight)
    loss = jnp.sum(weight_grid * crps) / (VARS * lat_total)
    grad_pred = (weight_grid[None] * (obs_sign / members - pair_sign * scale_pair)).astype(jnp.bfloat16)
    factor = POINTS / lat_total

    def backward(pair):
        member_rows, member_grad = pair
        normed, unit_rows, inv_std = normalize(member_rows, gain)
        grad_normed = jnp.dot(member_grad.T, weight, preferred_element_type=jnp.float32)
        grad_unit = grad_normed * gain[None, :]
        mean_one = lax.optimization_barrier(jnp.mean(grad_unit, axis=-1, keepdims=True))
        mean_two = lax.optimization_barrier(jnp.mean(grad_unit * unit_rows, axis=-1, keepdims=True))
        grad_rows = (factor * (inv_std * (grad_unit - mean_one - unit_rows * mean_two))).astype(jnp.bfloat16)
        part_weight = jnp.dot(member_grad, normed, preferred_element_type=jnp.float32)
        part_gain = lax.optimization_barrier(jnp.sum(grad_normed * unit_rows, axis=0))
        part_bias = lax.optimization_barrier(jnp.sum(member_grad.astype(jnp.float32), axis=1))
        return (grad_rows, part_weight, part_gain, part_bias)
    grad_fields, weight_parts, gain_parts, bias_parts = lax.map(backward, (fields, grad_pred))
    grad_weight = factor * lax.optimization_barrier(jnp.sum(weight_parts, axis=0))
    grad_gain = factor * lax.optimization_barrier(jnp.sum(gain_parts, axis=0))
    grad_bias = factor * lax.optimization_barrier(jnp.sum(bias_parts, axis=0))
    return (grad_fields, grad_weight, grad_gain, grad_bias, loss)
```

```python
import functools
import jax
import jax.numpy as jnp
from jax import lax
from jax.experimental import pallas as pl
from jax.experimental.pallas import tpu as pltpu
from jax.sharding import Mesh, PartitionSpec as P

soft_square = 0.01
norm_epsilon = 1e-05

V = 100
M = 8
D = 1024
LOCAL = 1024
LANES = 128
ROWS = 104
GAIN_ROW, MISC_ROW, LAT_ROW = 100, 101, 102
XC = ("x", "core")
YZ = ("y_lo", "y_hi", "z")
MEMBER = ("y_hi", "core")
VMEM_LIMIT = 20 * 1024 * 1024
f32, bf16 = jnp.float32, jnp.bfloat16
NT = (((1,), (1,)), ((), ()))
TN = (((0,), (0,)), ((), ()))


def params(**kw):
    return pltpu.CompilerParams(vmem_limit_bytes=VMEM_LIMIT, **kw)


def column(row):
    n = row.shape[1]
    if n < LANES:
        row = jnp.concatenate([row, jnp.zeros((1, LANES - n), row.dtype)], axis=1)
    return jnp.broadcast_to(row, (LANES, LANES)).T


def unit_of(values):
    row_mean = jnp.mean(values, axis=-1, keepdims=True)
    centred = values - row_mean
    inv_std = lax.rsqrt(jnp.mean(centred * centred, axis=-1, keepdims=True) + norm_epsilon)
    return centred * inv_std, inv_std


def forward_kernel(fields_ref, weight_ref, bias_ref, gain_ref, pred_ref, normed_ref, resid_ref):
    unit, _ = unit_of(fields_ref[...].astype(f32))
    scaled = unit * gain_ref[...]
    normed = scaled.astype(bf16)
    normed_ref[...] = normed
    resid_ref[...] = (scaled - normed.astype(f32)).astype(bf16)
    pred = lax.dot_general(weight_ref[...], normed, NT, preferred_element_type=f32)
    bias = column(bias_ref[...])[:V]
    for k in range(pred_ref.shape[0]):
        pred_ref[k] = pred[:, k * LANES : (k + 1) * LANES] + bias


def forward(fields, weight, bias, gain, tile=256):
    slots = tile // LANES
    return pl.pallas_call(
        forward_kernel,
        grid=(LOCAL // tile,),
        in_specs=[
            pl.BlockSpec((tile, D), lambda i: (i, 0)),
            pl.BlockSpec((V, D), lambda i: (0, 0)),
            pl.BlockSpec((1, V), lambda i: (0, 0)),
            pl.BlockSpec((1, D), lambda i: (0, 0)),
        ],
        out_specs=[
            pl.BlockSpec((slots, V, LANES), lambda i: (i, 0, 0)),
            pl.BlockSpec((tile, D), lambda i: (i, 0)),
            pl.BlockSpec((tile, D), lambda i: (i, 0)),
        ],
        out_shape=[
            jax.ShapeDtypeStruct((M, V, LANES), f32),
            jax.ShapeDtypeStruct((LOCAL, D), bf16),
            jax.ShapeDtypeStruct((LOCAL, D), bf16),
        ],
        compiler_params=params(),
        cost_estimate=pl.CostEstimate(flops=2 * V * D * LOCAL, bytes_accessed=8 << 20, transcendentals=0),
    )(fields, weight, bias, gain)


def pair_kernel(slot_ref, pred_ref, obs_ref, lat_ref, vw_ref, grad_ref, loss_ref):
    del slot_ref
    vw = column(vw_ref[...])
    lat = lat_ref[...].reshape(1, LANES)
    loss = jnp.zeros((8, LANES), f32)
    for start in range(0, V, 8):
        rows = min(8, V - start)
        part = slice(start, start + rows)
        obs = obs_ref[part].astype(f32)
        pred = [pred_ref[m, part] for m in range(M)]
        sign = [None] * M
        pair_abs = None
        obs_abs = None
        for m in range(M):
            gap = pred[m] - obs
            square = gap * gap + soft_square
            inverse = lax.rsqrt(square)
            size = square * inverse
            obs_abs = size if obs_abs is None else obs_abs + size
            sign[m] = gap * inverse * float(M - 1)
        for i in range(M):
            for j in range(i + 1, M):
                gap = pred[i] - pred[j]
                square = gap * gap + soft_square
                inverse = lax.rsqrt(square)
                size = square * inverse
                pair_abs = size if pair_abs is None else pair_abs + size
                term = gap * inverse
                sign[i] = sign[i] - term
                sign[j] = sign[j] + term
        scale = vw[part] * lat
        crps = obs_abs * (1.0 / M) - pair_abs * (1.0 / (M * (M - 1)))
        crps = crps * scale
        if rows < 8:
            crps = jnp.concatenate([crps, jnp.zeros((8 - rows, LANES), f32)], axis=0)
        loss = loss + crps
        scale = scale * (1.0 / (M * (M - 1)))
        for m in range(M):
            grad_ref[m, part] = sign[m] * scale
    loss_ref[...] = loss


def pair(slot, pred, observed, lat, var_weight):
    return pl.pallas_call(
        pair_kernel,
        grid_spec=pltpu.PrefetchScalarGridSpec(
            num_scalar_prefetch=1,
            grid=(1,),
            in_specs=[
                pl.BlockSpec((M, V, LANES), lambda i, s: (0, 0, 0)),
                pl.BlockSpec((V, LANES), lambda i, s: (0, s[0])),
                pl.BlockSpec((1, 1, LANES), lambda i, s: (s[0], 0, 0)),
                pl.BlockSpec((1, V), lambda i, s: (0, 0)),
            ],
            out_specs=[
                pl.BlockSpec((M, V, LANES), lambda i, s: (0, 0, 0)),
                pl.BlockSpec((8, LANES), lambda i, s: (0, 0)),
            ],
        ),
        out_shape=[
            jax.ShapeDtypeStruct((M, V, LANES), f32),
            jax.ShapeDtypeStruct((8, LANES), f32),
        ],
        compiler_params=params(),
    )(slot, pred, observed, lat, var_weight)


def weight_kernel(grad_ref, normed_ref, resid_ref, weight_ref, gain_ref, lat_ref, loss_ref, out_ref, total_ref, rest_ref, sums_ref):
    step = pl.program_id(0)
    slots = grad_ref.shape[0]
    grad = jnp.concatenate([grad_ref[k] for k in range(slots)], axis=1).astype(bf16)
    total = jnp.dot(grad, normed_ref[...], preferred_element_type=f32)
    rest = jnp.dot(grad, resid_ref[...], preferred_element_type=f32)
    ones = jnp.ones((8, grad.shape[1]), bf16)
    sums = lax.dot_general(ones, grad, NT, preferred_element_type=f32)

    @pl.when(step == 0)
    def _():
        total_ref[...] = total
        rest_ref[...] = rest
        sums_ref[...] = sums

    @pl.when(step > 0)
    def _():
        total_ref[...] += total
        rest_ref[...] += rest
        sums_ref[...] += sums

    @pl.when(step == pl.num_programs(0) - 1)
    def _():
        total = total_ref[...]
        part = weight_ref[...].astype(f32) * (total + rest_ref[...])
        part_gain = jnp.sum(part, axis=0, keepdims=True) / gain_ref[...]
        lane = lax.broadcasted_iota(jnp.int32, (1, LANES), 1)
        bias_row = jnp.concatenate([sums_ref[0:1], jnp.zeros((1, LANES - V), f32)], axis=1)
        loss = jnp.sum(loss_ref[...], keepdims=True)
        misc = jnp.where(lane == V, loss, bias_row)
        lat = jnp.broadcast_to(jnp.sum(lat_ref[...], keepdims=True), (1, LANES))
        tail = jnp.concatenate([misc, lat, jnp.zeros((1, LANES), f32)], axis=0)
        for k in range(M):
            cols = slice(k * LANES, (k + 1) * LANES)
            out_ref[k, :V] = total[:, cols]
            out_ref[k, V:] = jnp.concatenate([part_gain[:, cols], tail], axis=0)


def weight_part(grad, normed, resid, weight, gain, lat, loss, tile=256):
    slots = tile // LANES
    return pl.pallas_call(
        weight_kernel,
        grid=(LOCAL // tile,),
        in_specs=[
            pl.BlockSpec((slots, V, LANES), lambda i: (i, 0, 0)),
            pl.BlockSpec((tile, D), lambda i: (i, 0)),
            pl.BlockSpec((tile, D), lambda i: (i, 0)),
            pl.BlockSpec((V, D), lambda i: (0, 0)),
            pl.BlockSpec((1, D), lambda i: (0, 0)),
            pl.BlockSpec((M, LANES), lambda i: (0, 0)),
            pl.BlockSpec((8, LANES), lambda i: (0, 0)),
        ],
        out_specs=pl.BlockSpec((M, ROWS, LANES), lambda i: (0, 0, 0)),
        out_shape=jax.ShapeDtypeStruct((M, ROWS, LANES), f32),
        scratch_shapes=[pltpu.VMEM((V, D), f32), pltpu.VMEM((V, D), f32), pltpu.VMEM((8, V), f32)],
        compiler_params=params(),
    )(grad, normed, resid, weight, gain, lat, loss)


def fold_kernel(parts_ref, out_ref):
    total = parts_ref[0]
    for k in range(1, M):
        total = total + parts_ref[k]
    total = jnp.concatenate([total, jnp.zeros((LANES - ROWS, LANES), f32)], axis=0)
    out_ref[...] = total.T


def fold(parts):
    return pl.pallas_call(
        fold_kernel,
        out_shape=jax.ShapeDtypeStruct((LANES, LANES), f32),
        compiler_params=params(),
    )(parts)


def share_kernel(parts_ref, out_ref, lat_ref):
    total = jnp.sum(parts_ref[...], axis=0)
    out_ref[...] = jnp.broadcast_to(total[None], out_ref.shape)
    lat_ref[...] = jnp.broadcast_to(total[0:1, LAT_ROW : LAT_ROW + 1] * (1.0 / M), (8, LANES))


def share(parts):
    return pl.pallas_call(
        share_kernel,
        out_shape=[
            jax.ShapeDtypeStruct(parts.shape, f32),
            jax.ShapeDtypeStruct((8, LANES), f32),
        ],
        compiler_params=params(),
    )(parts)


def spread_kernel(parts_ref, out_ref):
    total = parts_ref[...].T[:ROWS]
    out_ref[...] = jnp.broadcast_to(total[None], out_ref.shape)


def spread(parts):
    return pl.pallas_call(
        spread_kernel,
        out_shape=jax.ShapeDtypeStruct((M, ROWS, LANES), f32),
        compiler_params=params(),
    )(parts)


def finish_kernel(points_total, parts_ref, weight_ref, gain_ref, bias_ref, loss_ref):
    lat_total = parts_ref[0, LAT_ROW : LAT_ROW + 1, 0:1] * (1.0 / M)
    factor = points_total / lat_total
    for k in range(M):
        cols = slice(k * LANES, (k + 1) * LANES)
        weight_ref[:, cols] = parts_ref[k, :V] * factor
        gain_ref[:, cols] = parts_ref[k, GAIN_ROW : GAIN_ROW + 1] * factor
    misc = parts_ref[0, MISC_ROW : MISC_ROW + 1]
    bias_ref[...] = misc[:, :V] * factor
    loss_ref[...] = misc[:, V : V + 1] / (V * lat_total)


def finish(parts, points_total):
    return pl.pallas_call(
        functools.partial(finish_kernel, points_total),
        out_shape=[
            jax.ShapeDtypeStruct((V, D), f32),
            jax.ShapeDtypeStruct((1, D), f32),
            jax.ShapeDtypeStruct((1, V), f32),
            jax.ShapeDtypeStruct((1, 1), f32),
        ],
        compiler_params=params(),
    )(parts)


def fields_kernel(points_total, fields_ref, grad_ref, weight_ref, gain_ref, lat_ref, out_ref):
    unit, inv_std = unit_of(fields_ref[...].astype(f32))
    slots = grad_ref.shape[0]
    grad = jnp.concatenate([grad_ref[k] for k in range(slots)], axis=1).astype(bf16)
    grad_normed = lax.dot_general(grad, weight_ref[...], TN, preferred_element_type=f32)
    grad_unit = grad_normed * gain_ref[...]
    mean_one = jnp.mean(grad_unit, axis=-1, keepdims=True)
    mean_two = jnp.mean(grad_unit * unit, axis=-1, keepdims=True)
    factor = points_total / lat_ref[0:1, 0:1]
    out_ref[...] = ((factor * inv_std) * (grad_unit - mean_one - unit * mean_two)).astype(bf16)


def fields_part(fields, grad, weight, gain, lat_total, points_total, tile=256):
    slots = tile // LANES
    return pl.pallas_call(
        functools.partial(fields_kernel, points_total),
        grid=(LOCAL // tile,),
        in_specs=[
            pl.BlockSpec((tile, D), lambda i: (i, 0)),
            pl.BlockSpec((slots, V, LANES), lambda i: (i, 0, 0)),
            pl.BlockSpec((V, D), lambda i: (0, 0)),
            pl.BlockSpec((1, D), lambda i: (0, 0)),
            pl.BlockSpec((8, LANES), lambda i: (0, 0)),
        ],
        out_specs=pl.BlockSpec((tile, D), lambda i: (i, 0)),
        out_shape=jax.ShapeDtypeStruct((LOCAL, D), bf16),
        compiler_params=params(),
        cost_estimate=pl.CostEstimate(flops=2 * V * D * LOCAL, bytes_accessed=5 << 20, transcendentals=0),
    )(fields, grad, weight, gain, lat_total)


def swap(array, axes):
    return lax.all_to_all(array, axes, split_axis=0, concat_axis=0, tiled=True)


def shards(points_total, fields, observed, lat_weight, var_weight, weight, bias, gain):
    fields = fields.reshape(LOCAL, D)
    gain_row = gain.reshape(1, D)
    slot = lax.axis_index(MEMBER).astype(jnp.int32).reshape(1)
    pred, normed, resid = forward(fields, weight, bias.reshape(1, V), gain_row)
    pred = swap(pred, MEMBER)
    grad, loss = pair(slot, pred, observed, lat_weight.reshape(M, 1, LANES), var_weight.reshape(1, V))
    grad = swap(grad, MEMBER)
    parts = weight_part(grad, normed, resid, weight, gain_row, lat_weight.reshape(M, LANES), loss)
    parts = swap(parts, XC)
    parts = fold(parts).reshape(64, 2, LANES)
    parts = swap(parts, YZ)
    parts, lat_total = share(parts)
    parts = swap(parts, YZ)
    grad_fields = fields_part(fields, grad, weight, gain_row, lat_total, points_total)
    parts = spread(parts.reshape(LANES, LANES))
    parts = swap(parts, XC)
    grad_weight, grad_gain, grad_bias, loss = finish(parts, points_total)
    return (
        grad_fields.reshape(1, LOCAL, D),
        grad_weight,
        grad_gain.reshape(D),
        grad_bias.reshape(V),
        loss.reshape(()),
    )


def solution(mesh):
    devices = mesh.devices.reshape(4, 2, 8, 4, 2)
    fine = Mesh(devices, ("x", "y_lo", "z", "y_hi", "core"))
    grid = ("x", "y_lo", "z")
    points_total = float(LOCAL * 64)
    return jax.shard_map(
        functools.partial(shards, points_total),
        mesh=fine,
        in_specs=(P(MEMBER, grid, None), P(None, grid), P(grid), P(), P(), P(), P()),
        out_specs=(P(MEMBER, grid, None), P(), P(), P(), P()),
        check_vma=False,
    )
```

```python
import functools
import jax
import jax.numpy as jnp
from jax import lax
from jax.experimental import pallas as pl
from jax.experimental.pallas import tpu as pltpu
from jax.sharding import Mesh, PartitionSpec as P

soft_square = 0.01
norm_epsilon = 1e-05

V = 100
M = 8
D = 1024
LOCAL = 1024
CHIPS = 256
LANES = 128
TILE = 256
ROWS = 104
GAIN_ROW, MISC_ROW, LAT_ROW = 100, 101, 102
GRID = ("x", "y_lo", "z")
MEMBER = ("y_hi", "core")
CHIP = ("x", "y_lo", "z", "y_hi")
VMEM_LIMIT = 16 * 1024 * 1024
WHOLE_VMEM = 60 * 1024 * 1024
RESIDUAL_VMEM = 62 * 1024 * 1024
VMEM = pl.BlockSpec(memory_space=pltpu.VMEM)
SMEM = pl.BlockSpec(memory_space=pltpu.SMEM)
HBM = pl.BlockSpec(memory_space=pltpu.HBM)
f32, bf16 = jnp.float32, jnp.bfloat16
NT = (((1,), (1,)), ((), ()))
TN = (((0,), (0,)), ((), ()))


def params(limit=VMEM_LIMIT):
    return pltpu.CompilerParams(vmem_limit_bytes=limit)


def column(row):
    n = row.shape[1]
    if n < LANES:
        row = jnp.concatenate([row, jnp.zeros((1, LANES - n), row.dtype)], axis=1)
    return jnp.broadcast_to(row, (LANES, LANES)).T


def unit_of(values):
    row_mean = jnp.mean(values, axis=-1, keepdims=True)
    centred = values - row_mean
    inv_std = lax.rsqrt(jnp.mean(centred * centred, axis=-1, keepdims=True) + norm_epsilon)
    return centred * inv_std, inv_std


def forward_kernel(fields_hbm, weight_hbm, bias_hbm, gain_hbm, pred_hbm, normed_hbm,
                   fields_ref, weight_ref, bias_ref, gain_ref, pred_ref, normed_ref, in_sems, out_sems):
    tiles = LOCAL // TILE
    slots = TILE // LANES
    rows = [pl.ds(t * TILE, TILE) for t in range(tiles)]
    small = [
        pltpu.make_async_copy(gain_hbm, gain_ref, in_sems.at[tiles]),
        pltpu.make_async_copy(weight_hbm, weight_ref, in_sems.at[tiles + 1]),
        pltpu.make_async_copy(bias_hbm, bias_ref, in_sems.at[tiles + 2]),
    ]
    large = [
        pltpu.make_async_copy(fields_hbm.at[rows[t]], fields_ref.at[rows[t]], in_sems.at[t])
        for t in range(tiles)
    ]
    large[0].start()
    for copy in small:
        copy.start()
    for copy in large[1:]:
        copy.start()
    back = []
    for t in range(tiles):
        large[t].wait()
        if t == 0:
            for copy in small:
                copy.wait()
            bias = column(bias_ref[...])[:V]
        unit, _ = unit_of(fields_ref[rows[t]].astype(f32))
        normed = (unit * gain_ref[...]).astype(bf16)
        normed_ref[rows[t]] = normed
        pred = lax.dot_general(weight_ref[...], normed, NT, preferred_element_type=f32)
        for k in range(slots):
            pred_ref[t * slots + k] = pred[:, k * LANES : (k + 1) * LANES] + bias
        here = pl.ds(t * slots, slots)
        back.append(pltpu.make_async_copy(pred_ref.at[here], pred_hbm.at[here], out_sems.at[t, 0]))
        back.append(pltpu.make_async_copy(normed_ref.at[rows[t]], normed_hbm.at[rows[t]], out_sems.at[t, 1]))
        back[-2].start()
        back[-1].start()
    for copy in back:
        copy.wait()


def forward(fields, weight, bias, gain):
    tiles = LOCAL // TILE
    return pl.pallas_call(
        forward_kernel,
        in_specs=[HBM] * 4,
        out_specs=[HBM] * 2,
        out_shape=[
            jax.ShapeDtypeStruct((M, V, LANES), f32),
            jax.ShapeDtypeStruct((LOCAL, D), bf16),
        ],
        scratch_shapes=[
            pltpu.VMEM((LOCAL, D), bf16),
            pltpu.VMEM((V, D), bf16),
            pltpu.VMEM((1, V), f32),
            pltpu.VMEM((1, D), f32),
            pltpu.VMEM((M, V, LANES), f32),
            pltpu.VMEM((LOCAL, D), bf16),
            pltpu.SemaphoreType.DMA((tiles + 3,)),
            pltpu.SemaphoreType.DMA((tiles, 2)),
        ],
        compiler_params=params(WHOLE_VMEM),
        cost_estimate=pl.CostEstimate(flops=2 * V * D * LOCAL, bytes_accessed=6 << 20, transcendentals=0),
    )(fields, weight, bias, gain)


def residual_kernel(fields_ref, gain_ref, normed_ref, out_ref):
    unit, _ = unit_of(fields_ref[...].astype(f32))
    out_ref[...] = (unit * gain_ref[...] - normed_ref[...].astype(f32)).astype(bf16)


def residual(fields, gain, normed):
    block = pl.BlockSpec((TILE, D), lambda i: (i, 0))
    return pl.pallas_call(
        residual_kernel,
        grid=(LOCAL // TILE,),
        in_specs=[block, pl.BlockSpec((1, D), lambda i: (0, 0)), block],
        out_specs=block,
        out_shape=jax.ShapeDtypeStruct((LOCAL, D), bf16),
        compiler_params=params(RESIDUAL_VMEM),
        cost_estimate=pl.CostEstimate(flops=12 * D * LOCAL, bytes_accessed=6 << 20, transcendentals=0),
    )(fields, gain, normed)


def pair_kernel(slot_ref, pred_ref, obs_ref, lat_ref, vw_ref, grad_ref, loss_ref):
    count = pred_ref.shape[1]
    here = pl.ds(pl.multiple_of(slot_ref[0] * LANES, LANES), LANES)
    vw = column(vw_ref[...])
    observed = obs_ref[:, here].astype(f32)
    lat = lat_ref[pl.ds(slot_ref[0], 1), :]
    loss = jnp.zeros((8, LANES), f32)
    for start in range(0, count, 8):
        rows = min(8, count - start)
        part = slice(start, start + rows)
        obs = observed[part]
        pred = [pred_ref[m, part] for m in range(M)]
        sign = [None] * M
        pair_abs = None
        obs_abs = None
        for m in range(M):
            gap = pred[m] - obs
            square = gap * gap + soft_square
            inverse = lax.rsqrt(square)
            size = square * inverse
            obs_abs = size if obs_abs is None else obs_abs + size
            sign[m] = gap * inverse * float(M - 1)
        for i in range(M):
            for j in range(i + 1, M):
                gap = pred[i] - pred[j]
                square = gap * gap + soft_square
                inverse = lax.rsqrt(square)
                size = square * inverse
                pair_abs = size if pair_abs is None else pair_abs + size
                term = gap * inverse
                sign[i] = sign[i] - term
                sign[j] = sign[j] + term
        scale = vw[part] * lat
        crps = obs_abs * (1.0 / M) - pair_abs * (1.0 / (M * (M - 1)))
        crps = crps * scale
        if rows < 8:
            crps = jnp.concatenate([crps, jnp.zeros((8 - rows, LANES), f32)], axis=0)
        loss = loss + crps
        scale = scale * (1.0 / (M * (M - 1)))
        for m in range(M):
            grad_ref[m, part] = sign[m] * scale
    loss_ref[...] = loss


def pair(slot, pred, observed, lat, var_weight):
    return pl.pallas_call(
        pair_kernel,
        in_specs=[SMEM] + [VMEM] * 4,
        out_specs=[pl.BlockSpec(pred.shape, lambda: (0, 0, 0)), VMEM],
        out_shape=[
            jax.ShapeDtypeStruct(pred.shape, f32),
            jax.ShapeDtypeStruct((8, LANES), f32),
        ],
        compiler_params=params(),
        cost_estimate=pl.CostEstimate(flops=1 << 20, bytes_accessed=1 << 19, transcendentals=0),
    )(slot, pred, observed, lat, var_weight)


def weight_kernel(grad_hbm, weight_hbm, gain_hbm, lat_hbm, loss_hbm, normed_hbm, resid_hbm, out_ref,
                  grad_ref, weight_ref, gain_ref, lat_ref, loss_ref, normed_ref, resid_ref, small_sems, sems):
    tiles = LOCAL // TILE
    slots = TILE // LANES
    small = [
        pltpu.make_async_copy(grad_hbm, grad_ref, small_sems.at[0]),
        pltpu.make_async_copy(loss_hbm, loss_ref, small_sems.at[1]),
        pltpu.make_async_copy(lat_hbm, lat_ref, small_sems.at[2]),
        pltpu.make_async_copy(weight_hbm, weight_ref, small_sems.at[3]),
        pltpu.make_async_copy(gain_hbm, gain_ref, small_sems.at[4]),
    ]
    for copy in small:
        copy.start()
    copies = []
    for t in range(tiles):
        rows = pl.ds(t * TILE, TILE)
        copies.append((
            pltpu.make_async_copy(normed_hbm.at[rows], normed_ref.at[rows], sems.at[t, 0]),
            pltpu.make_async_copy(resid_hbm.at[rows], resid_ref.at[rows], sems.at[t, 1]),
        ))
    for copy, _ in copies:
        copy.start()
    for _, copy in copies:
        copy.start()
    for copy in small:
        copy.wait()
    grads = [
        jnp.concatenate([grad_ref[t * slots + k] for k in range(slots)], axis=1).astype(bf16)
        for t in range(tiles)
    ]
    ones = jnp.ones((8, LOCAL), bf16)
    sums = lax.dot_general(ones, jnp.concatenate(grads, axis=1), NT, preferred_element_type=f32)
    loss = jnp.sum(loss_ref[...], keepdims=True)
    lane = lax.broadcasted_iota(jnp.int32, (1, D), 1)
    misc = jnp.concatenate([sums[0:1], jnp.zeros((1, D - V), f32)], axis=1)
    misc = jnp.where(lane == V, loss, misc)
    lat = jnp.broadcast_to(jnp.sum(lat_ref[...], keepdims=True), (1, D))
    total = jnp.zeros((V, D), f32)
    for t in range(tiles):
        copies[t][0].wait()
        rows = pl.ds(t * TILE, TILE)
        total = total + jnp.dot(grads[t], normed_ref[rows], preferred_element_type=f32)
    rest = jnp.zeros((V, D), f32)
    for t in range(tiles):
        copies[t][1].wait()
        rows = pl.ds(t * TILE, TILE)
        rest = rest + jnp.dot(grads[t], resid_ref[rows], preferred_element_type=f32)
    part_gain = jnp.sum(weight_ref[...].astype(f32) * (total + rest), axis=0, keepdims=True) / gain_ref[...]
    out_ref[:V] = total
    out_ref[V:] = jnp.concatenate([part_gain, misc, lat, jnp.zeros((1, D), f32)], axis=0)


def weight_part(grad, weight, gain, lat, loss, normed, resid):
    return pl.pallas_call(
        weight_kernel,
        in_specs=[HBM] * 7,
        out_specs=VMEM,
        out_shape=jax.ShapeDtypeStruct((ROWS, D), f32),
        scratch_shapes=[
            pltpu.VMEM((M, V, LANES), f32),
            pltpu.VMEM((V, D), bf16),
            pltpu.VMEM((1, D), f32),
            pltpu.VMEM((M, LANES), f32),
            pltpu.VMEM((8, LANES), f32),
            pltpu.VMEM((LOCAL, D), bf16),
            pltpu.VMEM((LOCAL, D), bf16),
            pltpu.SemaphoreType.DMA((5,)),
            pltpu.SemaphoreType.DMA((LOCAL // TILE, 2)),
        ],
        compiler_params=params(WHOLE_VMEM),
        cost_estimate=pl.CostEstimate(flops=4 * V * D * LOCAL, bytes_accessed=4 << 20, transcendentals=0),
    )(grad, weight, gain, lat, loss, normed, resid)


def fold_kernel(core_ref, parts_ref, out_ref):
    half = D // 2
    for k in range(half // LANES):
        start = pl.multiple_of(core_ref[0] * half + k * LANES, LANES)
        total = parts_ref[0, :, pl.ds(start, LANES)] + parts_ref[1, :, pl.ds(start, LANES)]
        total = jnp.concatenate([total, jnp.zeros((LANES - ROWS, LANES), f32)], axis=0)
        out_ref[k * LANES : (k + 1) * LANES] = total.T


def fold(core, parts):
    return pl.pallas_call(
        fold_kernel,
        in_specs=[SMEM, VMEM],
        out_specs=VMEM,
        out_shape=jax.ShapeDtypeStruct((D // 2, LANES), f32),
        compiler_params=params(),
    )(core, parts)


def share_kernel(parts_ref, out_ref, lat_ref):
    total = jnp.sum(parts_ref[...].reshape(D // 16, 8, LANES), axis=0)
    total = total + jnp.concatenate([total[4:], total[:4]], axis=0)
    total = total + jnp.concatenate([total[2:], total[:2]], axis=0)
    out_ref[...] = jnp.broadcast_to(total[None], (D // 16, 8, LANES)).reshape(D // 2, LANES)
    lat_ref[...] = jnp.broadcast_to(total[0:1, LAT_ROW : LAT_ROW + 1] * (1.0 / M), (8, LANES))


def share(parts):
    return pl.pallas_call(
        share_kernel,
        in_specs=[VMEM],
        out_specs=[VMEM, VMEM],
        out_shape=[
            jax.ShapeDtypeStruct((D // 2, LANES), f32),
            jax.ShapeDtypeStruct((8, LANES), f32),
        ],
        compiler_params=params(),
    )(parts)


def finish_kernel(points_total, parts_ref, weight_ref, gain_ref, bias_ref, loss_ref):
    lat_total = parts_ref[0:1, LAT_ROW : LAT_ROW + 1] * (1.0 / M)
    factor = points_total / lat_total
    for k in range(D // LANES):
        cols = slice(k * LANES, (k + 1) * LANES)
        block = parts_ref[cols].T
        weight_ref[:, cols] = block[:V] * factor
        gain_ref[:, cols] = block[GAIN_ROW : GAIN_ROW + 1] * factor
        if k == 0:
            misc = block[MISC_ROW : MISC_ROW + 1]
            bias_ref[...] = misc[:, :V] * factor
            loss_ref[...] = misc[:, V : V + 1] / (V * lat_total)


def finish(parts, points_total):
    return pl.pallas_call(
        functools.partial(finish_kernel, points_total),
        in_specs=[VMEM],
        out_shape=[
            jax.ShapeDtypeStruct((V, D), f32),
            jax.ShapeDtypeStruct((1, D), f32),
            jax.ShapeDtypeStruct((1, V), f32),
            jax.ShapeDtypeStruct((1, 1), f32),
        ],
        compiler_params=params(),
    )(parts)


def fields_kernel(points_total, fields_ref, grad_ref, weight_ref, gain_ref, lat_ref, out_ref):
    unit, inv_std = unit_of(fields_ref[...].astype(f32))
    slots = grad_ref.shape[0]
    grad = jnp.concatenate([grad_ref[k] for k in range(slots)], axis=1).astype(bf16)
    grad_normed = lax.dot_general(grad, weight_ref[...], TN, preferred_element_type=f32)
    grad_unit = grad_normed * gain_ref[...]
    mean_one = jnp.mean(grad_unit, axis=-1, keepdims=True)
    mean_two = jnp.mean(grad_unit * unit, axis=-1, keepdims=True)
    factor = points_total / lat_ref[0:1, 0:1]
    out_ref[...] = ((factor * inv_std) * (grad_unit - mean_one - unit * mean_two)).astype(bf16)


def fields_part(fields, grad, weight, gain, lat_total, points_total):
    slots = TILE // LANES
    return pl.pallas_call(
        functools.partial(fields_kernel, points_total),
        grid=(LOCAL // TILE,),
        in_specs=[
            pl.BlockSpec((TILE, D), lambda i: (i, 0)),
            pl.BlockSpec((slots, V, LANES), lambda i: (i, 0, 0)),
            pl.BlockSpec((V, D), lambda i: (0, 0)),
            pl.BlockSpec((1, D), lambda i: (0, 0)),
            pl.BlockSpec((8, LANES), lambda i: (0, 0)),
        ],
        out_specs=pl.BlockSpec((TILE, D), lambda i: (i, 0)),
        out_shape=jax.ShapeDtypeStruct((LOCAL, D), bf16),
        compiler_params=params(),
        cost_estimate=pl.CostEstimate(flops=2 * V * D * LOCAL, bytes_accessed=12 << 20, transcendentals=0),
    )(fields, grad, weight, gain, lat_total)


def swap(array, axes):
    return lax.all_to_all(array, axes, split_axis=0, concat_axis=0, tiled=True)


def shards(points_total, fields, observed, lat_weight, var_weight, weight, bias, gain):
    fields = fields.reshape(LOCAL, D)
    gain_row = gain.reshape(1, D)
    vw_row = var_weight.reshape(1, V)
    lat = lat_weight.reshape(M, LANES)
    slot = lax.axis_index(MEMBER).astype(jnp.int32).reshape(1)
    core = lax.axis_index("core").astype(jnp.int32).reshape(1)
    pred, normed = forward(fields, weight, bias.reshape(1, V), gain_row)
    pred = swap(pred, MEMBER)
    resid = residual(fields, gain_row, normed)
    pred, resid = lax.optimization_barrier((pred, resid))
    grad, loss = pair(slot, pred, observed, lat, vw_row)
    grad = swap(grad, MEMBER)
    sums = weight_part(grad, weight, gain_row, lat, loss, normed, resid)
    sums = lax.all_gather(sums, "core")
    sums = fold(core, sums)
    sums = swap(sums.reshape(CHIPS, 2, LANES), CHIP)
    sums, lat_total = share(sums.reshape(D // 2, LANES))
    sums = swap(sums.reshape(CHIPS, 2, LANES), CHIP)
    grad_fields = fields_part(fields, grad, weight, gain_row, lat_total, points_total)
    sums = lax.all_gather(sums.reshape(D // 2, LANES), "core", tiled=True)
    grad_weight, grad_gain, grad_bias, loss = finish(sums, points_total)
    return (
        grad_fields.reshape(1, LOCAL, D),
        grad_weight,
        grad_gain.reshape(D),
        grad_bias.reshape(V),
        loss.reshape(()),
    )


def solution(mesh):
    devices = mesh.devices.reshape(4, 2, 8, 4, 2)
    fine = Mesh(devices, ("x", "y_lo", "z", "y_hi", "core"))
    points_total = float(LOCAL * mesh.shape["grid"])
    return jax.shard_map(
        functools.partial(shards, points_total),
        mesh=fine,
        in_specs=(P(MEMBER, GRID, None), P(None, GRID), P(GRID), P(), P(), P(), P()),
        out_specs=(P(MEMBER, GRID, None), P(), P(), P(), P()),
        check_vma=False,
    )
```

```python
import functools
import jax
import jax.numpy as jnp
from jax import lax
from jax.experimental import pallas as pl
from jax.experimental.pallas import tpu as pltpu
from jax.sharding import Mesh, PartitionSpec as P

soft_square = 0.01
norm_epsilon = 1e-05

V = 100
M = 8
D = 1024
LOCAL = 1024
CHIPS = 256
LANES = 128
TILE = 256
ROWS = 104
GAIN_ROW, MISC_ROW, LAT_ROW = 100, 101, 102
GRID = ("x", "y_lo", "z")
MEMBER = ("y_hi", "core")
CHIP = ("x", "y_lo", "z", "y_hi")
VMEM_LIMIT = 16 * 1024 * 1024
FORWARD_VMEM = 60 * 1024 * 1024
RESIDUAL_VMEM = 60 * 1024 * 1024
WEIGHT_VMEM = 50 * 1024 * 1024
VMEM = pl.BlockSpec(memory_space=pltpu.VMEM)
SMEM = pl.BlockSpec(memory_space=pltpu.SMEM)
HBM = pl.BlockSpec(memory_space=pltpu.HBM)
f32, bf16 = jnp.float32, jnp.bfloat16
NT = (((1,), (1,)), ((), ()))
TN = (((0,), (0,)), ((), ()))


def params(limit=VMEM_LIMIT):
    return pltpu.CompilerParams(vmem_limit_bytes=limit)


def column(row):
    n = row.shape[1]
    if n < LANES:
        row = jnp.concatenate([row, jnp.zeros((1, LANES - n), row.dtype)], axis=1)
    return jnp.broadcast_to(row, (LANES, LANES)).T


def unit_of(values):
    row_mean = jnp.mean(values, axis=-1, keepdims=True)
    centred = values - row_mean
    inv_std = lax.rsqrt(jnp.mean(centred * centred, axis=-1, keepdims=True) + norm_epsilon)
    return centred * inv_std, inv_std


def forward_kernel(fields_hbm, weight_hbm, bias_hbm, gain_hbm, pred_hbm, normed_hbm,
                   fields_ref, weight_ref, bias_ref, gain_ref, pred_ref, normed_ref, in_sems, out_sems):
    rows = [pl.ds(t * LANES, LANES) for t in range(M)]
    small = [
        pltpu.make_async_copy(gain_hbm, gain_ref, in_sems.at[M]),
        pltpu.make_async_copy(weight_hbm, weight_ref, in_sems.at[M + 1]),
        pltpu.make_async_copy(bias_hbm, bias_ref, in_sems.at[M + 2]),
    ]
    large = [
        pltpu.make_async_copy(fields_hbm.at[rows[t]], fields_ref.at[rows[t]], in_sems.at[t])
        for t in range(M)
    ]
    large[0].start()
    for copy in small:
        copy.start()
    for copy in large[1:]:
        copy.start()
    back = []
    for t in range(M):
        large[t].wait()
        unit, _ = unit_of(fields_ref[rows[t]].astype(f32))
        if t == 0:
            for copy in small:
                copy.wait()
            bias = column(bias_ref[...])[:V]
        normed = (unit * gain_ref[...]).astype(bf16)
        normed_ref[rows[t]] = normed
        back.append(pltpu.make_async_copy(normed_ref.at[rows[t]], normed_hbm.at[rows[t]], out_sems.at[t, 1]))
        back[-1].start()
        pred = lax.dot_general(weight_ref[...], normed, NT, preferred_element_type=f32)
        pred_ref[t] = pred + bias
        back.append(pltpu.make_async_copy(pred_ref.at[t], pred_hbm.at[t], out_sems.at[t, 0]))
        back[-1].start()
    for copy in back:
        copy.wait()


def forward(fields, weight, bias, gain):
    return pl.pallas_call(
        forward_kernel,
        in_specs=[HBM] * 4,
        out_specs=[HBM, HBM],
        out_shape=[
            jax.ShapeDtypeStruct((M, V, LANES), f32),
            jax.ShapeDtypeStruct((LOCAL, D), bf16),
        ],
        scratch_shapes=[
            pltpu.VMEM((LOCAL, D), bf16),
            pltpu.VMEM((V, D), bf16),
            pltpu.VMEM((1, V), f32),
            pltpu.VMEM((1, D), f32),
            pltpu.VMEM((M, V, LANES), f32),
            pltpu.VMEM((LOCAL, D), bf16),
            pltpu.SemaphoreType.DMA((M + 3,)),
            pltpu.SemaphoreType.DMA((M, 2)),
        ],
        compiler_params=params(FORWARD_VMEM),
        cost_estimate=pl.CostEstimate(flops=2 * V * D * LOCAL, bytes_accessed=6 << 20, transcendentals=0),
    )(fields, weight, bias, gain)


def residual_kernel(fields_ref, gain_ref, normed_ref, out_ref):
    unit, _ = unit_of(fields_ref[...].astype(f32))
    out_ref[...] = (unit * gain_ref[...] - normed_ref[...].astype(f32)).astype(bf16)


def residual(fields, gain, normed):
    block = pl.BlockSpec((TILE, D), lambda i: (i, 0))
    return pl.pallas_call(
        residual_kernel,
        grid=(LOCAL // TILE,),
        in_specs=[block, pl.BlockSpec((1, D), lambda i: (0, 0)), block],
        out_specs=block,
        out_shape=jax.ShapeDtypeStruct((LOCAL, D), bf16),
        compiler_params=params(RESIDUAL_VMEM),
        cost_estimate=pl.CostEstimate(flops=12 * D * LOCAL, bytes_accessed=6 << 20, transcendentals=0),
    )(fields, gain, normed)


def pair_kernel(slot_ref, pred_ref, obs_ref, lat_ref, vw_ref, grad_ref, loss_ref):
    count = pred_ref.shape[1]
    here = pl.ds(pl.multiple_of(slot_ref[0] * LANES, LANES), LANES)
    vw = column(vw_ref[...])
    observed = obs_ref[:, here].astype(f32)
    lat = lat_ref[pl.ds(slot_ref[0], 1), :]
    loss = jnp.zeros((8, LANES), f32)
    for start in range(0, count, 8):
        rows = min(8, count - start)
        part = slice(start, start + rows)
        obs = observed[part]
        pred = [pred_ref[m, part] for m in range(M)]
        sign = [None] * M
        pair_abs = None
        obs_abs = None
        for m in range(M):
            gap = pred[m] - obs
            square = gap * gap + soft_square
            inverse = lax.rsqrt(square)
            size = square * inverse
            obs_abs = size if obs_abs is None else obs_abs + size
            sign[m] = gap * inverse * float(M - 1)
        for i in range(M):
            for j in range(i + 1, M):
                gap = pred[i] - pred[j]
                square = gap * gap + soft_square
                inverse = lax.rsqrt(square)
                size = square * inverse
                pair_abs = size if pair_abs is None else pair_abs + size
                term = gap * inverse
                sign[i] = sign[i] - term
                sign[j] = sign[j] + term
        scale = vw[part] * lat
        crps = obs_abs * (1.0 / M) - pair_abs * (1.0 / (M * (M - 1)))
        crps = crps * scale
        if rows < 8:
            crps = jnp.concatenate([crps, jnp.zeros((8 - rows, LANES), f32)], axis=0)
        loss = loss + crps
        scale = scale * (1.0 / (M * (M - 1)))
        for m in range(M):
            grad_ref[m, part] = sign[m] * scale
    loss_ref[...] = loss


def pair(slot, pred, observed, lat, var_weight):
    return pl.pallas_call(
        pair_kernel,
        in_specs=[SMEM] + [VMEM] * 4,
        out_specs=[pl.BlockSpec(pred.shape, lambda: (0, 0, 0)), VMEM],
        out_shape=[
            jax.ShapeDtypeStruct(pred.shape, f32),
            jax.ShapeDtypeStruct((8, LANES), f32),
        ],
        compiler_params=params(),
        cost_estimate=pl.CostEstimate(flops=1 << 20, bytes_accessed=1 << 19, transcendentals=0),
    )(slot, pred, observed, lat, var_weight)


def weight_kernel(grad_ref, weight_ref, gain_ref, lat_ref, loss_ref, normed_ref, resid_hbm, out_ref, resid_ref, sems):
    tiles = LOCAL // TILE
    copies = [
        pltpu.make_async_copy(
            resid_hbm.at[pl.ds(t * TILE, TILE)], resid_ref.at[pl.ds(t * TILE, TILE)], sems.at[t]
        )
        for t in range(tiles)
    ]
    for copy in copies:
        copy.start()
    grad = jnp.concatenate([grad_ref[k] for k in range(M)], axis=1).astype(bf16)
    ones = jnp.ones((8, LOCAL), bf16)
    sums = lax.dot_general(ones, grad, NT, preferred_element_type=f32)
    loss = jnp.sum(loss_ref[...], keepdims=True)
    lane = lax.broadcasted_iota(jnp.int32, (1, D), 1)
    misc = jnp.concatenate([sums[0:1], jnp.zeros((1, D - V), f32)], axis=1)
    misc = jnp.where(lane == V, loss, misc)
    lat = jnp.broadcast_to(jnp.sum(lat_ref[...], keepdims=True), (1, D))
    out_ref[:V] = jnp.dot(grad, normed_ref[...], preferred_element_type=f32)
    rest = jnp.zeros((V, D), f32)
    for t in range(tiles):
        copies[t].wait()
        rows = slice(t * TILE, (t + 1) * TILE)
        rest = rest + jnp.dot(grad[:, rows], resid_ref[rows], preferred_element_type=f32)
    part_gain = weight_ref[...].astype(f32) * (out_ref[:V] + rest)
    part_gain = jnp.sum(part_gain, axis=0, keepdims=True) / gain_ref[...]
    out_ref[V:] = jnp.concatenate([part_gain, misc, lat, jnp.zeros((1, D), f32)], axis=0)


def weight_part(grad, weight, gain, lat, loss, normed, resid):
    return pl.pallas_call(
        weight_kernel,
        in_specs=[VMEM] * 6 + [HBM],
        out_specs=VMEM,
        out_shape=jax.ShapeDtypeStruct((ROWS, D), f32),
        scratch_shapes=[
            pltpu.VMEM((LOCAL, D), bf16),
            pltpu.SemaphoreType.DMA((LOCAL // TILE,)),
        ],
        compiler_params=params(WEIGHT_VMEM),
        cost_estimate=pl.CostEstimate(flops=4 * V * D * LOCAL, bytes_accessed=4 << 20, transcendentals=0),
    )(grad, weight, gain, lat, loss, normed, resid)


def fold_kernel(core_ref, parts_ref, out_ref):
    half = D // 2
    for k in range(half // LANES):
        start = pl.multiple_of(core_ref[0] * half + k * LANES, LANES)
        total = parts_ref[0, :, pl.ds(start, LANES)] + parts_ref[1, :, pl.ds(start, LANES)]
        total = jnp.concatenate([total, jnp.zeros((LANES - ROWS, LANES), f32)], axis=0)
        out_ref[k * LANES : (k + 1) * LANES] = total.T


def fold(core, parts):
    return pl.pallas_call(
        fold_kernel,
        in_specs=[SMEM, VMEM],
        out_specs=VMEM,
        out_shape=jax.ShapeDtypeStruct((D // 2, LANES), f32),
        compiler_params=params(),
    )(core, parts)


def share_kernel(parts_ref, out_ref, lat_ref):
    total = jnp.sum(parts_ref[...].reshape(D // 16, 8, LANES), axis=0)
    total = total + jnp.concatenate([total[4:], total[:4]], axis=0)
    total = total + jnp.concatenate([total[2:], total[:2]], axis=0)
    out_ref[...] = jnp.broadcast_to(total[None], (D // 16, 8, LANES)).reshape(D // 2, LANES)
    lat_ref[...] = jnp.broadcast_to(total[0:1, LAT_ROW : LAT_ROW + 1] * (1.0 / M), (8, LANES))


def share(parts):
    return pl.pallas_call(
        share_kernel,
        in_specs=[VMEM],
        out_specs=[VMEM, VMEM],
        out_shape=[
            jax.ShapeDtypeStruct((D // 2, LANES), f32),
            jax.ShapeDtypeStruct((8, LANES), f32),
        ],
        compiler_params=params(),
    )(parts)


def finish_kernel(points_total, parts_ref, weight_ref, gain_ref, bias_ref, loss_ref):
    lat_total = parts_ref[0:1, LAT_ROW : LAT_ROW + 1] * (1.0 / M)
    factor = points_total / lat_total
    for k in range(D // LANES):
        cols = slice(k * LANES, (k + 1) * LANES)
        block = parts_ref[cols].T
        weight_ref[:, cols] = block[:V] * factor
        gain_ref[:, cols] = block[GAIN_ROW : GAIN_ROW + 1] * factor
        if k == 0:
            misc = block[MISC_ROW : MISC_ROW + 1]
            bias_ref[...] = misc[:, :V] * factor
            loss_ref[...] = misc[:, V : V + 1] / (V * lat_total)


def finish(parts, points_total):
    return pl.pallas_call(
        functools.partial(finish_kernel, points_total),
        in_specs=[VMEM],
        out_shape=[
            jax.ShapeDtypeStruct((V, D), f32),
            jax.ShapeDtypeStruct((1, D), f32),
            jax.ShapeDtypeStruct((1, V), f32),
            jax.ShapeDtypeStruct((1, 1), f32),
        ],
        compiler_params=params(),
    )(parts)


def fields_kernel(points_total, fields_ref, grad_ref, weight_ref, gain_ref, lat_ref, out_ref):
    unit, inv_std = unit_of(fields_ref[...].astype(f32))
    slots = grad_ref.shape[0]
    grad = jnp.concatenate([grad_ref[k] for k in range(slots)], axis=1).astype(bf16)
    grad_normed = lax.dot_general(grad, weight_ref[...], TN, preferred_element_type=f32)
    grad_unit = grad_normed * gain_ref[...]
    mean_one = jnp.mean(grad_unit, axis=-1, keepdims=True)
    mean_two = jnp.mean(grad_unit * unit, axis=-1, keepdims=True)
    factor = points_total / lat_ref[0:1, 0:1]
    out_ref[...] = ((factor * inv_std) * (grad_unit - mean_one - unit * mean_two)).astype(bf16)


def fields_part(fields, grad, weight, gain, lat_total, points_total):
    slots = TILE // LANES
    return pl.pallas_call(
        functools.partial(fields_kernel, points_total),
        grid=(LOCAL // TILE,),
        in_specs=[
            pl.BlockSpec((TILE, D), lambda i: (i, 0)),
            pl.BlockSpec((slots, V, LANES), lambda i: (i, 0, 0)),
            pl.BlockSpec((V, D), lambda i: (0, 0)),
            pl.BlockSpec((1, D), lambda i: (0, 0)),
            pl.BlockSpec((8, LANES), lambda i: (0, 0)),
        ],
        out_specs=pl.BlockSpec((TILE, D), lambda i: (i, 0)),
        out_shape=jax.ShapeDtypeStruct((LOCAL, D), bf16),
        compiler_params=params(),
        cost_estimate=pl.CostEstimate(flops=2 * V * D * LOCAL, bytes_accessed=12 << 20, transcendentals=0),
    )(fields, grad, weight, gain, lat_total)


def swap(array, axes):
    return lax.all_to_all(array, axes, split_axis=0, concat_axis=0, tiled=True)


def shards(points_total, fields, observed, lat_weight, var_weight, weight, bias, gain):
    fields = fields.reshape(LOCAL, D)
    gain_row = gain.reshape(1, D)
    vw_row = var_weight.reshape(1, V)
    lat = lat_weight.reshape(M, LANES)
    slot = lax.axis_index(MEMBER).astype(jnp.int32).reshape(1)
    core = lax.axis_index("core").astype(jnp.int32).reshape(1)
    pred, normed = forward(fields, weight, bias.reshape(1, V), gain_row)
    pred = swap(pred, MEMBER)
    resid = residual(fields, gain_row, normed)
    pred, resid = lax.optimization_barrier((pred, resid))
    grad, loss = pair(slot, pred, observed, lat, vw_row)
    grad = swap(grad, MEMBER)
    sums = weight_part(grad, weight, gain_row, lat, loss, normed, resid)
    sums = lax.all_gather(sums, "core")
    sums = fold(core, sums)
    sums = swap(sums.reshape(CHIPS, 2, LANES), CHIP)
    sums, lat_total = share(sums.reshape(D // 2, LANES))
    sums = swap(sums.reshape(CHIPS, 2, LANES), CHIP)
    grad_fields = fields_part(fields, grad, weight, gain_row, lat_total, points_total)
    sums = lax.all_gather(sums.reshape(D // 2, LANES), "core", tiled=True)
    grad_weight, grad_gain, grad_bias, loss = finish(sums, points_total)
    return (
        grad_fields.reshape(1, LOCAL, D),
        grad_weight,
        grad_gain.reshape(D),
        grad_bias.reshape(V),
        loss.reshape(()),
    )


def solution(mesh):
    devices = mesh.devices.reshape(4, 2, 8, 4, 2)
    fine = Mesh(devices, ("x", "y_lo", "z", "y_hi", "core"))
    points_total = float(LOCAL * mesh.shape["grid"])
    return jax.shard_map(
        functools.partial(shards, points_total),
        mesh=fine,
        in_specs=(P(MEMBER, GRID, None), P(None, GRID), P(GRID), P(), P(), P(), P()),
        out_specs=(P(MEMBER, GRID, None), P(), P(), P(), P()),
        check_vma=False,
    )
```

```python
import functools
import jax
import jax.numpy as jnp
from jax import lax
from jax.experimental import pallas as pl
from jax.experimental.pallas import tpu as pltpu
from jax.sharding import Mesh, PartitionSpec as P

soft_square = 0.01
norm_epsilon = 1e-05

V = 100
M = 8
D = 1024
LOCAL = 1024
CHIPS = 256
LANES = 128
TILE = 256
BLOCK = 32
PAIRS = 4
PADDED = 104
ROWS = 104
GAIN_ROW, MISC_ROW, LAT_ROW = 100, 101, 102
GRID = ("x", "y_lo", "z")
MEMBER = ("y_hi", "core")
CHIP = ("x", "y_lo", "z", "y_hi")
VMEM_LIMIT = 16 * 1024 * 1024
FORWARD_VMEM = 60 * 1024 * 1024
RESIDUAL_VMEM = 60 * 1024 * 1024
WEIGHT_VMEM = 50 * 1024 * 1024
VMEM = pl.BlockSpec(memory_space=pltpu.VMEM)
SMEM = pl.BlockSpec(memory_space=pltpu.SMEM)
HBM = pl.BlockSpec(memory_space=pltpu.HBM)
f32, bf16 = jnp.float32, jnp.bfloat16
NT = (((1,), (1,)), ((), ()))
TN = (((0,), (0,)), ((), ()))


def params(limit=VMEM_LIMIT):
    return pltpu.CompilerParams(vmem_limit_bytes=limit)


def column(row):
    n = row.shape[1]
    if n < LANES:
        row = jnp.concatenate([row, jnp.zeros((1, LANES - n), row.dtype)], axis=1)
    return jnp.broadcast_to(row, (LANES, LANES)).T


def unit_of(values):
    row_mean = jnp.mean(values, axis=-1, keepdims=True)
    centred = values - row_mean
    inv_std = lax.rsqrt(jnp.mean(centred * centred, axis=-1, keepdims=True) + norm_epsilon)
    return centred * inv_std, inv_std


def scaled_rows(fields_ref, rows, gain):
    unit, _ = unit_of(fields_ref[rows].astype(f32))
    return unit * gain


def forward_kernel(fields_hbm, weight_hbm, bias_hbm, gain_hbm, pred_hbm,
                   fields_ref, weight_ref, bias_ref, gain_ref, pred_ref, normed_ref, in_sems, out_sems):
    tiles = LOCAL // TILE
    slots = TILE // LANES
    rows = [pl.ds(t * TILE, TILE) for t in range(tiles)]
    small = [
        pltpu.make_async_copy(gain_hbm, gain_ref, in_sems.at[tiles]),
        pltpu.make_async_copy(weight_hbm, weight_ref, in_sems.at[tiles + 1]),
        pltpu.make_async_copy(bias_hbm, bias_ref, in_sems.at[tiles + 2]),
    ]
    large = [
        pltpu.make_async_copy(fields_hbm.at[rows[t]], fields_ref.at[rows[t]], in_sems.at[t])
        for t in range(tiles)
    ]
    large[0].start()
    for copy in small:
        copy.start()
    for copy in large[1:]:
        copy.start()
    for copy in small:
        copy.wait()
    bias = column(bias_ref[...])[:V]
    spare = jnp.zeros((PADDED - V, LANES), f32)
    back = []
    for t in range(tiles):
        large[t].wait()
        for start in range(t * TILE, (t + 1) * TILE, BLOCK):
            block = slice(start, start + BLOCK)
            normed_ref[block] = scaled_rows(fields_ref, block, gain_ref[...]).astype(bf16)
        pred = lax.dot_general(weight_ref[...], normed_ref[rows[t]], NT, preferred_element_type=f32)
        for k in range(slots):
            pred_ref[t * slots + k, :V] = pred[:, k * LANES : (k + 1) * LANES] + bias
            pred_ref[t * slots + k, V:] = spare
        here = pl.ds(t * slots, slots)
        back.append(pltpu.make_async_copy(pred_ref.at[here], pred_hbm.at[here], out_sems.at[t]))
        back[-1].start()
    for copy in back:
        copy.wait()


def forward(fields, weight, bias, gain):
    tiles = LOCAL // TILE
    return pl.pallas_call(
        forward_kernel,
        in_specs=[HBM] * 4,
        out_specs=HBM,
        out_shape=jax.ShapeDtypeStruct((M, PADDED, LANES), f32),
        scratch_shapes=[
            pltpu.VMEM((LOCAL, D), bf16),
            pltpu.VMEM((V, D), bf16),
            pltpu.VMEM((1, V), f32),
            pltpu.VMEM((1, D), f32),
            pltpu.VMEM((M, PADDED, LANES), f32),
            pltpu.VMEM((LOCAL, D), bf16),
            pltpu.SemaphoreType.DMA((tiles + 3,)),
            pltpu.SemaphoreType.DMA((tiles,)),
        ],
        compiler_params=params(FORWARD_VMEM),
        cost_estimate=pl.CostEstimate(flops=2 * V * D * LOCAL, bytes_accessed=3 << 20, transcendentals=0),
    )(fields, weight, bias, gain)


def normed_kernel(fields_ref, gain_ref, normed_ref, resid_ref):
    for start in range(0, TILE, BLOCK):
        block = slice(start, start + BLOCK)
        scaled = scaled_rows(fields_ref, block, gain_ref[...])
        normed = scaled.astype(bf16)
        normed_ref[block] = normed
        resid_ref[block] = (scaled - normed.astype(f32)).astype(bf16)


def normed_parts(fields, gain):
    block = pl.BlockSpec((TILE, D), lambda i: (i, 0))
    return pl.pallas_call(
        normed_kernel,
        grid=(LOCAL // TILE,),
        in_specs=[block, pl.BlockSpec((1, D), lambda i: (0, 0))],
        out_specs=[block, block],
        out_shape=[jax.ShapeDtypeStruct((LOCAL, D), bf16)] * 2,
        compiler_params=params(RESIDUAL_VMEM),
        cost_estimate=pl.CostEstimate(flops=12 * D * LOCAL, bytes_accessed=6 << 20, transcendentals=0),
    )(fields, gain)


def pair_kernel(slot_ref, core_ref, pred_ref, obs_ref, lat_ref, vw_ref, grad_ref, loss_ref):
    here = pl.ds(pl.multiple_of(slot_ref[0] * LANES, LANES), LANES)
    vw = column(vw_ref[...])
    observed = obs_ref[:, here].astype(f32)
    lat = lat_ref[pl.ds(slot_ref[0], 1), :]
    loss = jnp.zeros((8, LANES), f32)
    for start in range(0, V, 8):
        rows = min(8, V - start)
        part = slice(start, start + rows)
        obs = observed[part]
        pred = [pred_ref[m % 2, m // 2, core_ref[0], part] for m in range(M)]
        sign = [None] * M
        pair_abs = None
        obs_abs = None
        for m in range(M):
            gap = pred[m] - obs
            square = gap * gap + soft_square
            inverse = lax.rsqrt(square)
            size = square * inverse
            obs_abs = size if obs_abs is None else obs_abs + size
            sign[m] = gap * inverse * float(M - 1)
        for i in range(M):
            for j in range(i + 1, M):
                gap = pred[i] - pred[j]
                square = gap * gap + soft_square
                inverse = lax.rsqrt(square)
                size = square * inverse
                pair_abs = size if pair_abs is None else pair_abs + size
                term = gap * inverse
                sign[i] = sign[i] - term
                sign[j] = sign[j] + term
        scale = vw[part] * lat
        crps = obs_abs * (1.0 / M) - pair_abs * (1.0 / (M * (M - 1)))
        crps = crps * scale
        if rows < 8:
            crps = jnp.concatenate([crps, jnp.zeros((8 - rows, LANES), f32)], axis=0)
        loss = loss + crps
        scale = scale * (1.0 / (M * (M - 1)))
        for m in range(M):
            grad_ref[m, part] = sign[m] * scale
    for m in range(M):
        grad_ref[m, V:] = jnp.zeros((PADDED - V, LANES), f32)
    loss_ref[...] = loss


def pair(slot, core, pred, observed, lat, var_weight):
    return pl.pallas_call(
        pair_kernel,
        in_specs=[SMEM] * 2 + [VMEM] * 4,
        out_specs=[VMEM] * 2,
        out_shape=[
            jax.ShapeDtypeStruct((M, PADDED, LANES), f32),
            jax.ShapeDtypeStruct((8, LANES), f32),
        ],
        compiler_params=params(),
        cost_estimate=pl.CostEstimate(flops=1 << 20, bytes_accessed=1 << 19, transcendentals=0),
    )(slot, core, pred, observed, lat, var_weight)


def weight_kernel(core_ref, grad_ref, weight_ref, gain_ref, lat_ref, loss_ref, normed_ref, resid_hbm, out_ref, resid_ref, sems):
    tiles = LOCAL // TILE
    copies = [
        pltpu.make_async_copy(
            resid_hbm.at[pl.ds(t * TILE, TILE)], resid_ref.at[pl.ds(t * TILE, TILE)], sems.at[t]
        )
        for t in range(tiles)
    ]
    for copy in copies:
        copy.start()
    grad = jnp.concatenate([grad_ref[k % 2, k // 2, core_ref[0], :V] for k in range(M)], axis=1).astype(bf16)
    ones = jnp.ones((8, LOCAL), bf16)
    sums = lax.dot_general(ones, grad, NT, preferred_element_type=f32)
    loss = jnp.sum(loss_ref[...], keepdims=True)
    lane = lax.broadcasted_iota(jnp.int32, (1, D), 1)
    misc = jnp.concatenate([sums[0:1], jnp.zeros((1, D - V), f32)], axis=1)
    misc = jnp.where(lane == V, loss, misc)
    lat = jnp.broadcast_to(jnp.sum(lat_ref[...], keepdims=True), (1, D))
    out_ref[:V] = jnp.dot(grad, normed_ref[...], preferred_element_type=f32)
    rest = jnp.zeros((V, D), f32)
    for t in range(tiles):
        copies[t].wait()
        rows = slice(t * TILE, (t + 1) * TILE)
        rest = rest + jnp.dot(grad[:, rows], resid_ref[rows], preferred_element_type=f32)
    part_gain = weight_ref[...].astype(f32) * (out_ref[:V] + rest)
    part_gain = jnp.sum(part_gain, axis=0, keepdims=True) / gain_ref[...]
    out_ref[V:] = jnp.concatenate([part_gain, misc, lat, jnp.zeros((1, D), f32)], axis=0)


def weight_part(core, grad, weight, gain, lat, loss, normed, resid):
    return pl.pallas_call(
        weight_kernel,
        in_specs=[SMEM] + [VMEM] * 6 + [HBM],
        out_specs=VMEM,
        out_shape=jax.ShapeDtypeStruct((ROWS, D), f32),
        scratch_shapes=[
            pltpu.VMEM((LOCAL, D), bf16),
            pltpu.SemaphoreType.DMA((LOCAL // TILE,)),
        ],
        compiler_params=params(WEIGHT_VMEM),
        cost_estimate=pl.CostEstimate(flops=4 * V * D * LOCAL, bytes_accessed=4 << 20, transcendentals=0),
    )(core, grad, weight, gain, lat, loss, normed, resid)


def fold_kernel(core_ref, parts_ref, out_ref):
    half = D // 2
    for k in range(half // LANES):
        start = pl.multiple_of(core_ref[0] * half + k * LANES, LANES)
        total = parts_ref[0, :, pl.ds(start, LANES)] + parts_ref[1, :, pl.ds(start, LANES)]
        total = jnp.concatenate([total, jnp.zeros((LANES - ROWS, LANES), f32)], axis=0)
        out_ref[k * LANES : (k + 1) * LANES] = total.T


def fold(core, parts):
    return pl.pallas_call(
        fold_kernel,
        in_specs=[SMEM, VMEM],
        out_specs=VMEM,
        out_shape=jax.ShapeDtypeStruct((D // 2, LANES), f32),
        compiler_params=params(),
    )(core, parts)


def share_kernel(parts_ref, out_ref, lat_ref):
    total = jnp.sum(parts_ref[...].reshape(D // 16, 8, LANES), axis=0)
    total = total + jnp.concatenate([total[4:], total[:4]], axis=0)
    total = total + jnp.concatenate([total[2:], total[:2]], axis=0)
    out_ref[...] = jnp.broadcast_to(total[None], (D // 16, 8, LANES)).reshape(D // 2, LANES)
    lat_ref[...] = jnp.broadcast_to(total[0:1, LAT_ROW : LAT_ROW + 1] * (1.0 / M), (8, LANES))


def share(parts):
    return pl.pallas_call(
        share_kernel,
        in_specs=[VMEM],
        out_specs=[VMEM, VMEM],
        out_shape=[
            jax.ShapeDtypeStruct((D // 2, LANES), f32),
            jax.ShapeDtypeStruct((8, LANES), f32),
        ],
        compiler_params=params(),
    )(parts)


def finish_kernel(points_total, parts_ref, weight_ref, gain_ref, bias_ref, loss_ref):
    lat_total = parts_ref[0:1, LAT_ROW : LAT_ROW + 1] * (1.0 / M)
    factor = points_total / lat_total
    for k in range(D // LANES):
        cols = slice(k * LANES, (k + 1) * LANES)
        block = parts_ref[cols].T
        weight_ref[:, cols] = block[:V] * factor
        gain_ref[:, cols] = block[GAIN_ROW : GAIN_ROW + 1] * factor
        if k == 0:
            misc = block[MISC_ROW : MISC_ROW + 1]
            bias_ref[...] = misc[:, :V] * factor
            loss_ref[...] = misc[:, V : V + 1] / (V * lat_total)


def finish(parts, points_total):
    return pl.pallas_call(
        functools.partial(finish_kernel, points_total),
        in_specs=[VMEM],
        out_shape=[
            jax.ShapeDtypeStruct((V, D), f32),
            jax.ShapeDtypeStruct((1, D), f32),
            jax.ShapeDtypeStruct((1, V), f32),
            jax.ShapeDtypeStruct((1, 1), f32),
        ],
        compiler_params=params(),
    )(parts)


def fields_kernel(points_total, core_ref, fields_ref, grad_ref, weight_ref, gain_ref, lat_ref, out_ref):
    del core_ref
    unit, inv_std = unit_of(fields_ref[...].astype(f32))
    grad = jnp.concatenate([grad_ref[0, 0, 0, :V], grad_ref[1, 0, 0, :V]], axis=1).astype(bf16)
    grad_normed = lax.dot_general(grad, weight_ref[...], TN, preferred_element_type=f32)
    grad_unit = grad_normed * gain_ref[...]
    mean_one = jnp.mean(grad_unit, axis=-1, keepdims=True)
    mean_two = jnp.mean(grad_unit * unit, axis=-1, keepdims=True)
    factor = points_total / lat_ref[0:1, 0:1]
    out_ref[...] = ((factor * inv_std) * (grad_unit - mean_one - unit * mean_two)).astype(bf16)


def fields_part(core, fields, grad, weight, gain, lat_total, points_total):
    return pl.pallas_call(
        functools.partial(fields_kernel, points_total),
        grid_spec=pltpu.PrefetchScalarGridSpec(
            num_scalar_prefetch=1,
            grid=(PAIRS,),
            in_specs=[
                pl.BlockSpec((TILE, D), lambda i, c: (i, 0)),
                pl.BlockSpec((2, 1, 1, PADDED, LANES), lambda i, c: (0, i, c[0], 0, 0)),
                pl.BlockSpec((V, D), lambda i, c: (0, 0)),
                pl.BlockSpec((1, D), lambda i, c: (0, 0)),
                pl.BlockSpec((8, LANES), lambda i, c: (0, 0)),
            ],
            out_specs=pl.BlockSpec((TILE, D), lambda i, c: (i, 0)),
        ),
        out_shape=jax.ShapeDtypeStruct((LOCAL, D), bf16),
        compiler_params=params(),
        cost_estimate=pl.CostEstimate(flops=2 * V * D * LOCAL, bytes_accessed=12 << 20, transcendentals=0),
    )(core, fields, grad, weight, gain, lat_total)


def swap(array, axes):
    return lax.all_to_all(array, axes, split_axis=0, concat_axis=0, tiled=True)


def exchange(array):
    return swap(array, "y_hi")


def both_cores(array):
    return lax.all_gather(array, "core").reshape(2, PAIRS, 2, PADDED, LANES)


def shards(points_total, fields, observed, lat_weight, var_weight, weight, bias, gain):
    fields = fields.reshape(LOCAL, D)
    gain_row = gain.reshape(1, D)
    vw_row = var_weight.reshape(1, V)
    lat = lat_weight.reshape(M, LANES)
    slot = lax.axis_index(MEMBER).astype(jnp.int32).reshape(1)
    core = lax.axis_index("core").astype(jnp.int32).reshape(1)
    pred = forward(fields, weight, bias.reshape(1, V), gain_row)
    pred = exchange(pred)
    normed, resid = normed_parts(fields, gain_row)
    pred, normed, resid = lax.optimization_barrier((pred, normed, resid))
    pred = both_cores(pred)
    grad, loss = pair(slot, core, pred, observed, lat, vw_row)
    grad = both_cores(exchange(grad))
    sums = weight_part(core, grad, weight, gain_row, lat, loss, normed, resid)
    sums = lax.all_gather(sums, "core")
    sums = fold(core, sums)
    sums = swap(sums.reshape(CHIPS, 2, LANES), CHIP)
    sums, lat_total = share(sums.reshape(D // 2, LANES))
    sums = swap(sums.reshape(CHIPS, 2, LANES), CHIP)
    grad_fields = fields_part(core, fields, grad, weight, gain_row, lat_total, points_total)
    sums = lax.all_gather(sums.reshape(D // 2, LANES), "core", tiled=True)
    grad_weight, grad_gain, grad_bias, loss = finish(sums, points_total)
    return (
        grad_fields.reshape(1, LOCAL, D),
        grad_weight,
        grad_gain.reshape(D),
        grad_bias.reshape(V),
        loss.reshape(()),
    )


def solution(mesh):
    devices = mesh.devices.reshape(4, 2, 8, 4, 2)
    fine = Mesh(devices, ("x", "y_lo", "z", "y_hi", "core"))
    points_total = float(LOCAL * mesh.shape["grid"])
    return jax.shard_map(
        functools.partial(shards, points_total),
        mesh=fine,
        in_specs=(P(MEMBER, GRID, None), P(None, GRID), P(GRID), P(), P(), P(), P()),
        out_specs=(P(MEMBER, GRID, None), P(), P(), P(), P()),
        check_vma=False,
    )
```

```python
import functools
import jax
import jax.numpy as jnp
from jax import lax
from jax.experimental import pallas as pl
from jax.experimental.pallas import tpu as pltpu
from jax.sharding import Mesh, PartitionSpec as P

soft_square = 0.01
norm_epsilon = 1e-05

V = 100
M = 8
D = 1024
LOCAL = 1024
CHIPS = 256
LANES = 128
TILE = 256
BLOCK = 32
ROWS = 104
GAIN_ROW, MISC_ROW, LAT_ROW = 100, 101, 102
GRID = ("x", "y_lo", "z")
MEMBER = ("y_hi", "core")
PLACE = ("core", "y_hi")
CHIP = ("x", "y_hi", "y_lo", "z")
VMEM_LIMIT = 16 * 1024 * 1024
FORWARD_VMEM = 60 * 1024 * 1024
RESIDUAL_VMEM = 60 * 1024 * 1024
WEIGHT_VMEM = 50 * 1024 * 1024
VMEM = pl.BlockSpec(memory_space=pltpu.VMEM)
SMEM = pl.BlockSpec(memory_space=pltpu.SMEM)
HBM = pl.BlockSpec(memory_space=pltpu.HBM)
f32, bf16, f8 = jnp.float32, jnp.bfloat16, jnp.float8_e4m3fn
RESIDUAL_SCALE = 512.0
NT = (((1,), (1,)), ((), ()))
TN = (((0,), (0,)), ((), ()))


def params(limit=VMEM_LIMIT):
    return pltpu.CompilerParams(vmem_limit_bytes=limit)


def column(row):
    n = row.shape[1]
    if n < LANES:
        row = jnp.concatenate([row, jnp.zeros((1, LANES - n), row.dtype)], axis=1)
    return jnp.broadcast_to(row, (LANES, LANES)).T


def unit_of(values):
    row_mean = jnp.mean(values, axis=-1, keepdims=True)
    centred = values - row_mean
    inv_std = lax.rsqrt(jnp.mean(centred * centred, axis=-1, keepdims=True) + norm_epsilon)
    return centred * inv_std, inv_std


def scaled_rows(fields_ref, rows, gain):
    unit, _ = unit_of(fields_ref[rows].astype(f32))
    return unit * gain


def forward_kernel(fields_hbm, weight_hbm, bias_hbm, gain_hbm, pred_hbm, normed_hbm,
                   fields_ref, weight_ref, bias_ref, gain_ref, pred_ref, normed_ref, in_sems, out_sems):
    tiles = LOCAL // TILE
    slots = TILE // LANES
    rows = [pl.ds(t * TILE, TILE) for t in range(tiles)]
    small = [
        pltpu.make_async_copy(gain_hbm, gain_ref, in_sems.at[tiles]),
        pltpu.make_async_copy(weight_hbm, weight_ref, in_sems.at[tiles + 1]),
        pltpu.make_async_copy(bias_hbm, bias_ref, in_sems.at[tiles + 2]),
    ]
    large = [
        pltpu.make_async_copy(fields_hbm.at[rows[t]], fields_ref.at[rows[t]], in_sems.at[t])
        for t in range(tiles)
    ]
    large[0].start()
    for copy in small:
        copy.start()
    for copy in large[1:]:
        copy.start()
    for copy in small:
        copy.wait()
    bias = column(bias_ref[...])[:V]
    back = []
    for t in range(tiles + 1):
        if t < tiles:
            large[t].wait()
            for start in range(t * TILE, (t + 1) * TILE, BLOCK):
                block = slice(start, start + BLOCK)
                normed_ref[block] = scaled_rows(fields_ref, block, gain_ref[...]).astype(bf16)
            back.append(pltpu.make_async_copy(normed_ref.at[rows[t]], normed_hbm.at[rows[t]], out_sems.at[t, 1]))
            back[-1].start()
        if t > 0:
            done = normed_ref[rows[t - 1]]
            pred = lax.dot_general(weight_ref[...], done, NT, preferred_element_type=f32)
            first = (t - 1) * slots
            for k in range(slots):
                pred_ref[first + k] = pred[:, k * LANES : (k + 1) * LANES] + bias
            here = pl.ds(first, slots)
            back.append(pltpu.make_async_copy(pred_ref.at[here], pred_hbm.at[here], out_sems.at[t - 1, 0]))
            back[-1].start()
    for copy in back:
        copy.wait()


def forward(fields, weight, bias, gain):
    tiles = LOCAL // TILE
    return pl.pallas_call(
        forward_kernel,
        in_specs=[HBM] * 4,
        out_specs=[HBM] * 2,
        out_shape=[
            jax.ShapeDtypeStruct((M, V, LANES), f32),
            jax.ShapeDtypeStruct((LOCAL, D), bf16),
        ],
        scratch_shapes=[
            pltpu.VMEM((LOCAL, D), bf16),
            pltpu.VMEM((V, D), bf16),
            pltpu.VMEM((1, V), f32),
            pltpu.VMEM((1, D), f32),
            pltpu.VMEM((M, V, LANES), f32),
            pltpu.VMEM((LOCAL, D), bf16),
            pltpu.SemaphoreType.DMA((tiles + 3,)),
            pltpu.SemaphoreType.DMA((tiles, 2)),
        ],
        compiler_params=params(FORWARD_VMEM),
        cost_estimate=pl.CostEstimate(flops=2 * V * D * LOCAL, bytes_accessed=3 << 20, transcendentals=0),
    )(fields, weight, bias, gain)


def residual_kernel(fields_ref, gain_ref, resid_ref):
    for start in range(0, TILE, BLOCK):
        block = slice(start, start + BLOCK)
        scaled = scaled_rows(fields_ref, block, gain_ref[...])
        rest = scaled - scaled.astype(bf16).astype(f32)
        resid_ref[block] = (rest * RESIDUAL_SCALE).astype(f8)


def residual(fields, gain):
    block = pl.BlockSpec((TILE, D), lambda i: (i, 0))
    return pl.pallas_call(
        residual_kernel,
        grid=(LOCAL // TILE,),
        in_specs=[block, pl.BlockSpec((1, D), lambda i: (0, 0))],
        out_specs=block,
        out_shape=jax.ShapeDtypeStruct((2 * LOCAL, D), f8),
        compiler_params=params(RESIDUAL_VMEM),
        cost_estimate=pl.CostEstimate(flops=12 * D * LOCAL, bytes_accessed=6 << 20, transcendentals=0),
    )(fields, gain)


def pair_kernel(slot_ref, pred_ref, obs_ref, lat_ref, vw_ref, grad_ref, loss_ref):
    here = pl.ds(pl.multiple_of(slot_ref[0] * LANES, LANES), LANES)
    vw = column(vw_ref[...])
    observed = obs_ref[:, here].astype(f32)
    lat = lat_ref[pl.ds(slot_ref[0], 1), :]
    loss = jnp.zeros((8, LANES), f32)
    for start in range(0, V, 8):
        rows = min(8, V - start)
        part = slice(start, start + rows)
        obs = observed[part]
        pred = [pred_ref[m, part] for m in range(M)]
        sign = [None] * M
        pair_abs = None
        obs_abs = None
        for m in range(M):
            gap = pred[m] - obs
            square = gap * gap + soft_square
            inverse = lax.rsqrt(square)
            size = square * inverse
            obs_abs = size if obs_abs is None else obs_abs + size
            sign[m] = gap * inverse * float(M - 1)
        for i in range(M):
            for j in range(i + 1, M):
                gap = pred[i] - pred[j]
                square = gap * gap + soft_square
                inverse = lax.rsqrt(square)
                size = square * inverse
                pair_abs = size if pair_abs is None else pair_abs + size
                term = gap * inverse
                sign[i] = sign[i] - term
                sign[j] = sign[j] + term
        scale = vw[part] * lat
        crps = obs_abs * (1.0 / M) - pair_abs * (1.0 / (M * (M - 1)))
        crps = crps * scale
        if rows < 8:
            crps = jnp.concatenate([crps, jnp.zeros((8 - rows, LANES), f32)], axis=0)
        loss = loss + crps
        scale = scale * (1.0 / (M * (M - 1)))
        for m in range(M):
            grad_ref[m, part] = sign[m] * scale
    loss_ref[...] = loss


def pair(slot, pred, observed, lat, var_weight):
    return pl.pallas_call(
        pair_kernel,
        in_specs=[SMEM] + [VMEM] * 4,
        out_specs=[VMEM] * 2,
        out_shape=[
            jax.ShapeDtypeStruct((M, V, LANES), f32),
            jax.ShapeDtypeStruct((8, LANES), f32),
        ],
        compiler_params=params(),
        cost_estimate=pl.CostEstimate(flops=1 << 20, bytes_accessed=1 << 19, transcendentals=0),
    )(slot, pred, observed, lat, var_weight)


def weight_kernel(grad_ref, weight_ref, gain_ref, lat_ref, loss_ref, normed_ref, resid_hbm, out_ref, resid_ref, sems):
    tiles = LOCAL // TILE
    copies = [
        pltpu.make_async_copy(
            resid_hbm.at[pl.ds(t * TILE, TILE)], resid_ref.at[pl.ds(t * TILE, TILE)], sems.at[t]
        )
        for t in range(tiles)
    ]
    for copy in copies:
        copy.start()
    grad = jnp.concatenate([grad_ref[k] for k in range(M)], axis=1).astype(bf16)
    ones = jnp.ones((8, LOCAL), bf16)
    sums = lax.dot_general(ones, grad, NT, preferred_element_type=f32)
    loss = jnp.sum(loss_ref[...], keepdims=True)
    lane = lax.broadcasted_iota(jnp.int32, (1, D), 1)
    misc = jnp.concatenate([sums[0:1], jnp.zeros((1, D - V), f32)], axis=1)
    misc = jnp.where(lane == V, loss, misc)
    lat = jnp.broadcast_to(jnp.sum(lat_ref[...], keepdims=True), (1, D))
    out_ref[:V] = jnp.dot(grad, normed_ref[...], preferred_element_type=f32)
    rest = jnp.zeros((V, D), f32)
    for t in range(tiles):
        copies[t].wait()
        rows = slice(t * TILE, (t + 1) * TILE)
        rest = rest + jnp.dot(grad[:, rows], resid_ref[rows].astype(bf16), preferred_element_type=f32)
    part_gain = weight_ref[...].astype(f32) * (out_ref[:V] + rest * (1.0 / RESIDUAL_SCALE))
    part_gain = jnp.sum(part_gain, axis=0, keepdims=True) / gain_ref[...]
    out_ref[V:] = jnp.concatenate([part_gain, misc, lat, jnp.zeros((1, D), f32)], axis=0)


def weight_part(grad, weight, gain, lat, loss, normed, resid):
    return pl.pallas_call(
        weight_kernel,
        in_specs=[VMEM] * 6 + [HBM],
        out_specs=VMEM,
        out_shape=jax.ShapeDtypeStruct((ROWS, D), f32),
        scratch_shapes=[
            pltpu.VMEM((LOCAL, D), f8),
            pltpu.SemaphoreType.DMA((LOCAL // TILE,)),
        ],
        compiler_params=params(WEIGHT_VMEM),
        cost_estimate=pl.CostEstimate(flops=4 * V * D * LOCAL, bytes_accessed=4 << 20, transcendentals=0),
    )(grad, weight, gain, lat, loss, normed, resid)


def fold_kernel(core_ref, parts_ref, out_ref):
    half = D // 2
    for k in range(half // LANES):
        start = pl.multiple_of(core_ref[0] * half + k * LANES, LANES)
        total = parts_ref[0, :, pl.ds(start, LANES)] + parts_ref[1, :, pl.ds(start, LANES)]
        total = jnp.concatenate([total, jnp.zeros((LANES - ROWS, LANES), f32)], axis=0)
        out_ref[k * LANES : (k + 1) * LANES] = total.T


def fold(core, parts):
    return pl.pallas_call(
        fold_kernel,
        in_specs=[SMEM, VMEM],
        out_specs=VMEM,
        out_shape=jax.ShapeDtypeStruct((D // 2, LANES), f32),
        compiler_params=params(),
    )(core, parts)


def share_kernel(parts_ref, out_ref, lat_ref):
    total = jnp.sum(parts_ref[...].reshape(D // 16, 8, LANES), axis=0)
    total = total + jnp.concatenate([total[4:], total[:4]], axis=0)
    total = total + jnp.concatenate([total[2:], total[:2]], axis=0)
    out_ref[...] = jnp.broadcast_to(total[None], (D // 16, 8, LANES)).reshape(D // 2, LANES)
    lat_ref[...] = jnp.broadcast_to(total[0:1, LAT_ROW : LAT_ROW + 1] * (1.0 / M), (8, LANES))


def share(parts):
    return pl.pallas_call(
        share_kernel,
        in_specs=[VMEM],
        out_specs=[VMEM, VMEM],
        out_shape=[
            jax.ShapeDtypeStruct((D // 2, LANES), f32),
            jax.ShapeDtypeStruct((8, LANES), f32),
        ],
        compiler_params=params(),
    )(parts)


def finish_kernel(points_total, parts_ref, weight_ref, gain_ref, bias_ref, loss_ref):
    lat_total = parts_ref[0:1, LAT_ROW : LAT_ROW + 1] * (1.0 / M)
    factor = points_total / lat_total
    for k in range(D // LANES):
        cols = slice(k * LANES, (k + 1) * LANES)
        block = parts_ref[cols].T
        weight_ref[:, cols] = block[:V] * factor
        gain_ref[:, cols] = block[GAIN_ROW : GAIN_ROW + 1] * factor
        if k == 0:
            misc = block[MISC_ROW : MISC_ROW + 1]
            bias_ref[...] = misc[:, :V] * factor
            loss_ref[...] = misc[:, V : V + 1] / (V * lat_total)


def finish(parts, points_total):
    return pl.pallas_call(
        functools.partial(finish_kernel, points_total),
        in_specs=[VMEM],
        out_shape=[
            jax.ShapeDtypeStruct((V, D), f32),
            jax.ShapeDtypeStruct((1, D), f32),
            jax.ShapeDtypeStruct((1, V), f32),
            jax.ShapeDtypeStruct((1, 1), f32),
        ],
        compiler_params=params(),
    )(parts)


def fields_kernel(points_total, fields_ref, grad_ref, weight_ref, gain_ref, lat_ref, out_ref):
    unit, inv_std = unit_of(fields_ref[...].astype(f32))
    slots = grad_ref.shape[0]
    grad = jnp.concatenate([grad_ref[k] for k in range(slots)], axis=1).astype(bf16)
    grad_normed = lax.dot_general(grad, weight_ref[...], TN, preferred_element_type=f32)
    grad_unit = grad_normed * gain_ref[...]
    mean_one = jnp.mean(grad_unit, axis=-1, keepdims=True)
    mean_two = jnp.mean(grad_unit * unit, axis=-1, keepdims=True)
    factor = points_total / lat_ref[0:1, 0:1]
    out_ref[...] = ((factor * inv_std) * (grad_unit - mean_one - unit * mean_two)).astype(bf16)


def fields_part(fields, grad, weight, gain, lat_total, points_total):
    slots = TILE // LANES
    return pl.pallas_call(
        functools.partial(fields_kernel, points_total),
        grid=(LOCAL // TILE,),
        in_specs=[
            pl.BlockSpec((TILE, D), lambda i: (i, 0)),
            pl.BlockSpec((slots, V, LANES), lambda i: (i, 0, 0)),
            pl.BlockSpec((V, D), lambda i: (0, 0)),
            pl.BlockSpec((1, D), lambda i: (0, 0)),
            pl.BlockSpec((8, LANES), lambda i: (0, 0)),
        ],
        out_specs=pl.BlockSpec((TILE, D), lambda i: (i, 0)),
        out_shape=jax.ShapeDtypeStruct((LOCAL, D), bf16),
        compiler_params=params(),
        cost_estimate=pl.CostEstimate(flops=2 * V * D * LOCAL, bytes_accessed=12 << 20, transcendentals=0),
    )(fields, grad, weight, gain, lat_total)


def swap(array, axes):
    return lax.all_to_all(array, axes, split_axis=0, concat_axis=0, tiled=True)


def shards(points_total, fields, observed, lat_weight, var_weight, weight, bias, gain):
    fields = fields.reshape(LOCAL, D)
    gain_row = gain.reshape(1, D)
    vw_row = var_weight.reshape(1, V)
    lat = lat_weight.reshape(M, LANES)
    slot = lax.axis_index(PLACE).astype(jnp.int32).reshape(1)
    core = lax.axis_index("core").astype(jnp.int32).reshape(1)
    pred, normed = forward(fields, weight, bias.reshape(1, V), gain_row)
    pred = swap(pred, PLACE)
    resid = residual(fields, gain_row)
    pred, resid = lax.optimization_barrier((pred, resid))
    grad, loss = pair(slot, pred, observed, lat, vw_row)
    grad = swap(grad, PLACE)
    sums = weight_part(grad, weight, gain_row, lat, loss, normed, resid)
    sums = lax.all_gather(sums, "core")
    sums = fold(core, sums)
    sums = swap(sums.reshape(CHIPS, 2, LANES), CHIP)
    sums, lat_total = share(sums.reshape(D // 2, LANES))
    sums = swap(sums.reshape(CHIPS, 2, LANES), CHIP)
    grad_fields = fields_part(fields, grad, weight, gain_row, lat_total, points_total)
    sums = lax.all_gather(sums.reshape(D // 2, LANES), "core", tiled=True)
    grad_weight, grad_gain, grad_bias, loss = finish(sums, points_total)
    return (
        grad_fields.reshape(1, LOCAL, D),
        grad_weight,
        grad_gain.reshape(D),
        grad_bias.reshape(V),
        loss.reshape(()),
    )


def solution(mesh):
    devices = mesh.devices.reshape(4, 2, 8, 4, 2)
    fine = Mesh(devices, ("x", "y_lo", "z", "y_hi", "core"))
    points_total = float(LOCAL * mesh.shape["grid"])
    return jax.shard_map(
        functools.partial(shards, points_total),
        mesh=fine,
        in_specs=(P(MEMBER, GRID, None), P(None, GRID), P(GRID), P(), P(), P(), P()),
        out_specs=(P(MEMBER, GRID, None), P(), P(), P(), P()),
        check_vma=False,
    )
```

```python
import functools
import jax
import jax.numpy as jnp
from jax import lax
from jax.experimental import pallas as pl
from jax.experimental.pallas import tpu as pltpu
from jax.sharding import Mesh, PartitionSpec as P

soft_square = 0.01
norm_epsilon = 1e-05

V = 100
M = 8
D = 1024
LOCAL = 1024
CHIPS = 256
LANES = 128
TILE = 256
BLOCK = 32
STEP = 512
ROWS = 104
GAIN_ROW, MISC_ROW, LAT_ROW = 100, 101, 102
GRID = ("x", "y_lo", "z")
MEMBER = ("y_hi", "core")
PLACE = ("core", "y_hi")
CHIP = ("x", "y_hi", "y_lo", "z")
VMEM_LIMIT = 16 * 1024 * 1024
FORWARD_VMEM = 60 * 1024 * 1024
RESIDUAL_VMEM = 60 * 1024 * 1024
WEIGHT_VMEM = 50 * 1024 * 1024
VMEM = pl.BlockSpec(memory_space=pltpu.VMEM)
SMEM = pl.BlockSpec(memory_space=pltpu.SMEM)
HBM = pl.BlockSpec(memory_space=pltpu.HBM)
f32, bf16, f8 = jnp.float32, jnp.bfloat16, jnp.float8_e4m3fn
RESIDUAL_SCALE = 512.0
NT = (((1,), (1,)), ((), ()))
TN = (((0,), (0,)), ((), ()))


def params(limit=VMEM_LIMIT):
    return pltpu.CompilerParams(vmem_limit_bytes=limit)


def column(row):
    n = row.shape[1]
    if n < LANES:
        row = jnp.concatenate([row, jnp.zeros((1, LANES - n), row.dtype)], axis=1)
    return jnp.broadcast_to(row, (LANES, LANES)).T


def unit_of(values):
    row_mean = jnp.mean(values, axis=-1, keepdims=True)
    centred = values - row_mean
    inv_std = lax.rsqrt(jnp.mean(centred * centred, axis=-1, keepdims=True) + norm_epsilon)
    return centred * inv_std, inv_std


def scaled_rows(fields_ref, rows, gain):
    unit, _ = unit_of(fields_ref[rows].astype(f32))
    return unit * gain


def forward_kernel(fields_hbm, weight_hbm, bias_hbm, gain_hbm, pred_hbm, normed_hbm,
                   fields_ref, weight_ref, bias_ref, gain_ref, pred_ref, normed_ref, in_sems, out_sems):
    tiles = LOCAL // TILE
    slots = TILE // LANES
    rows = [pl.ds(t * TILE, TILE) for t in range(tiles)]
    small = [
        pltpu.make_async_copy(gain_hbm, gain_ref, in_sems.at[tiles]),
        pltpu.make_async_copy(weight_hbm, weight_ref, in_sems.at[tiles + 1]),
        pltpu.make_async_copy(bias_hbm, bias_ref, in_sems.at[tiles + 2]),
    ]
    large = [
        pltpu.make_async_copy(fields_hbm.at[rows[t]], fields_ref.at[rows[t]], in_sems.at[t])
        for t in range(1, tiles)
    ]
    halves = [
        pltpu.make_async_copy(fields_hbm.at[half], fields_ref.at[half], sem)
        for half, sem in (
            (pl.ds(0, TILE // 2), in_sems.at[0]),
            (pl.ds(TILE // 2, TILE // 2), in_sems.at[tiles + 3]),
        )
    ]
    halves[0].start()
    for copy in small:
        copy.start()
    for copy in halves[1:] + large:
        copy.start()
    small[0].wait()
    back = []
    for t in range(tiles + 1):
        if t < tiles:
            if t > 0:
                large[t - 1].wait()
            for start in range(t * TILE, (t + 1) * TILE, BLOCK):
                if t == 0 and start % (TILE // 2) == 0:
                    halves[start // (TILE // 2)].wait()
                block = slice(start, start + BLOCK)
                normed_ref[block] = scaled_rows(fields_ref, block, gain_ref[...]).astype(bf16)
            back.append(pltpu.make_async_copy(normed_ref.at[rows[t]], normed_hbm.at[rows[t]], out_sems.at[t, 1]))
            back[-1].start()
        if t == 1:
            for copy in small[1:]:
                copy.wait()
            bias = column(bias_ref[...])[:V]
        if t > 0:
            done = normed_ref[rows[t - 1]]
            pred = lax.dot_general(weight_ref[...], done, NT, preferred_element_type=f32)
            first = (t - 1) * slots
            for k in range(slots):
                pred_ref[first + k] = pred[:, k * LANES : (k + 1) * LANES] + bias
            here = pl.ds(first, slots)
            back.append(pltpu.make_async_copy(pred_ref.at[here], pred_hbm.at[here], out_sems.at[t - 1, 0]))
            back[-1].start()
    for copy in back:
        copy.wait()


def forward(fields, weight, bias, gain):
    tiles = LOCAL // TILE
    return pl.pallas_call(
        forward_kernel,
        in_specs=[HBM] * 4,
        out_specs=[HBM] * 2,
        out_shape=[
            jax.ShapeDtypeStruct((M, V, LANES), f32),
            jax.ShapeDtypeStruct((LOCAL, D), bf16),
        ],
        scratch_shapes=[
            pltpu.VMEM((LOCAL, D), bf16),
            pltpu.VMEM((V, D), bf16),
            pltpu.VMEM((1, V), f32),
            pltpu.VMEM((1, D), f32),
            pltpu.VMEM((M, V, LANES), f32),
            pltpu.VMEM((LOCAL, D), bf16),
            pltpu.SemaphoreType.DMA((tiles + 4,)),
            pltpu.SemaphoreType.DMA((tiles, 2)),
        ],
        compiler_params=params(FORWARD_VMEM),
        cost_estimate=pl.CostEstimate(flops=2 * V * D * LOCAL, bytes_accessed=3 << 20, transcendentals=0),
    )(fields, weight, bias, gain)


def residual_kernel(fields_ref, gain_ref, resid_ref):
    for start in range(0, TILE, BLOCK):
        block = slice(start, start + BLOCK)
        scaled = scaled_rows(fields_ref, block, gain_ref[...])
        rest = scaled - scaled.astype(bf16).astype(f32)
        resid_ref[block] = (rest * RESIDUAL_SCALE).astype(f8)


def residual(fields, gain):
    block = pl.BlockSpec((TILE, D), lambda i: (i, 0))
    return pl.pallas_call(
        residual_kernel,
        grid=(LOCAL // TILE,),
        in_specs=[block, pl.BlockSpec((1, D), lambda i: (0, 0))],
        out_specs=block,
        out_shape=jax.ShapeDtypeStruct((2 * LOCAL, D), f8),
        compiler_params=params(RESIDUAL_VMEM),
        cost_estimate=pl.CostEstimate(flops=12 * D * LOCAL, bytes_accessed=6 << 20, transcendentals=0),
    )(fields, gain)


def pair_kernel(slot_ref, pred_ref, obs_ref, lat_ref, vw_ref, grad_ref, loss_ref):
    here = pl.ds(pl.multiple_of(slot_ref[0] * LANES, LANES), LANES)
    vw = column(vw_ref[...])
    observed = obs_ref[:, here].astype(f32)
    lat = lat_ref[pl.ds(slot_ref[0], 1), :]
    loss = jnp.zeros((8, LANES), f32)
    for start in range(0, V, 8):
        rows = min(8, V - start)
        part = slice(start, start + rows)
        obs = observed[part]
        pred = [pred_ref[m, part] for m in range(M)]
        sign = [None] * M
        pair_abs = None
        obs_abs = None
        for m in range(M):
            gap = pred[m] - obs
            square = gap * gap + soft_square
            inverse = lax.rsqrt(square)
            size = square * inverse
            obs_abs = size if obs_abs is None else obs_abs + size
            sign[m] = gap * inverse * float(M - 1)
        for i in range(M):
            for j in range(i + 1, M):
                gap = pred[i] - pred[j]
                square = gap * gap + soft_square
                inverse = lax.rsqrt(square)
                size = square * inverse
                pair_abs = size if pair_abs is None else pair_abs + size
                term = gap * inverse
                sign[i] = sign[i] - term
                sign[j] = sign[j] + term
        scale = vw[part] * lat
        crps = obs_abs * (1.0 / M) - pair_abs * (1.0 / (M * (M - 1)))
        crps = crps * scale
        if rows < 8:
            crps = jnp.concatenate([crps, jnp.zeros((8 - rows, LANES), f32)], axis=0)
        loss = loss + crps
        scale = scale * (1.0 / (M * (M - 1)))
        for m in range(M):
            grad_ref[m, part] = sign[m] * scale
    loss_ref[...] = loss


def pair(slot, pred, observed, lat, var_weight):
    return pl.pallas_call(
        pair_kernel,
        in_specs=[SMEM] + [VMEM] * 4,
        out_specs=[VMEM] * 2,
        out_shape=[
            jax.ShapeDtypeStruct((M, V, LANES), f32),
            jax.ShapeDtypeStruct((8, LANES), f32),
        ],
        compiler_params=params(),
        cost_estimate=pl.CostEstimate(flops=1 << 20, bytes_accessed=1 << 19, transcendentals=0),
    )(slot, pred, observed, lat, var_weight)


def weight_kernel(grad_ref, weight_ref, gain_ref, lat_ref, loss_ref, normed_ref, resid_hbm, out_ref, resid_ref, sems):
    tiles = LOCAL // STEP
    copies = [
        pltpu.make_async_copy(
            resid_hbm.at[pl.ds(t * STEP, STEP)], resid_ref.at[pl.ds(t * STEP, STEP)], sems.at[t]
        )
        for t in range(tiles)
    ]
    for copy in copies:
        copy.start()
    grad = jnp.concatenate([grad_ref[k] for k in range(M)], axis=1).astype(bf16)
    ones = jnp.ones((8, LOCAL), bf16)
    sums = lax.dot_general(ones, grad, NT, preferred_element_type=f32)
    loss = jnp.sum(loss_ref[...], keepdims=True)
    lane = lax.broadcasted_iota(jnp.int32, (1, D), 1)
    misc = jnp.concatenate([sums[0:1], jnp.zeros((1, D - V), f32)], axis=1)
    misc = jnp.where(lane == V, loss, misc)
    lat = jnp.broadcast_to(jnp.sum(lat_ref[...], keepdims=True), (1, D))
    out_ref[:V] = jnp.dot(grad, normed_ref[...], preferred_element_type=f32)
    rest = jnp.zeros((V, D), f32)
    for t in range(tiles):
        copies[t].wait()
        rows = slice(t * STEP, (t + 1) * STEP)
        rest = rest + jnp.dot(grad[:, rows], resid_ref[rows].astype(bf16), preferred_element_type=f32)
    part_gain = weight_ref[...].astype(f32) * (out_ref[:V] + rest * (1.0 / RESIDUAL_SCALE))
    part_gain = jnp.sum(part_gain, axis=0, keepdims=True) / gain_ref[...]
    out_ref[V:] = jnp.concatenate([part_gain, misc, lat, jnp.zeros((1, D), f32)], axis=0)


def weight_part(grad, weight, gain, lat, loss, normed, resid):
    return pl.pallas_call(
        weight_kernel,
        in_specs=[VMEM] * 6 + [HBM],
        out_specs=VMEM,
        out_shape=jax.ShapeDtypeStruct((ROWS, D), f32),
        scratch_shapes=[
            pltpu.VMEM((LOCAL, D), f8),
            pltpu.SemaphoreType.DMA((LOCAL // STEP,)),
        ],
        compiler_params=params(WEIGHT_VMEM),
        cost_estimate=pl.CostEstimate(flops=4 * V * D * LOCAL, bytes_accessed=4 << 20, transcendentals=0),
    )(grad, weight, gain, lat, loss, normed, resid)


def fold_kernel(core_ref, parts_ref, out_ref):
    half = D // 2
    for k in range(half // LANES):
        start = pl.multiple_of(core_ref[0] * half + k * LANES, LANES)
        total = parts_ref[0, :, pl.ds(start, LANES)] + parts_ref[1, :, pl.ds(start, LANES)]
        total = jnp.concatenate([total, jnp.zeros((LANES - ROWS, LANES), f32)], axis=0)
        out_ref[k * LANES : (k + 1) * LANES] = total.T


def fold(core, parts):
    return pl.pallas_call(
        fold_kernel,
        in_specs=[SMEM, VMEM],
        out_specs=VMEM,
        out_shape=jax.ShapeDtypeStruct((D // 2, LANES), f32),
        compiler_params=params(),
    )(core, parts)


def share_kernel(parts_ref, out_ref, lat_ref):
    total = jnp.sum(parts_ref[...].reshape(D // 16, 8, LANES), axis=0)
    total = total + jnp.concatenate([total[4:], total[:4]], axis=0)
    total = total + jnp.concatenate([total[2:], total[:2]], axis=0)
    out_ref[...] = jnp.broadcast_to(total[None], (D // 16, 8, LANES)).reshape(D // 2, LANES)
    lat_ref[...] = jnp.broadcast_to(total[0:1, LAT_ROW : LAT_ROW + 1] * (1.0 / M), (8, LANES))


def share(parts):
    return pl.pallas_call(
        share_kernel,
        in_specs=[VMEM],
        out_specs=[VMEM, VMEM],
        out_shape=[
            jax.ShapeDtypeStruct((D // 2, LANES), f32),
            jax.ShapeDtypeStruct((8, LANES), f32),
        ],
        compiler_params=params(),
    )(parts)


def finish_kernel(points_total, parts_ref, weight_ref, gain_ref, bias_ref, loss_ref):
    lat_total = parts_ref[0:1, LAT_ROW : LAT_ROW + 1] * (1.0 / M)
    factor = points_total / lat_total
    for k in range(D // LANES):
        cols = slice(k * LANES, (k + 1) * LANES)
        block = parts_ref[cols].T
        weight_ref[:, cols] = block[:V] * factor
        gain_ref[:, cols] = block[GAIN_ROW : GAIN_ROW + 1] * factor
        if k == 0:
            misc = block[MISC_ROW : MISC_ROW + 1]
            bias_ref[...] = misc[:, :V] * factor
            loss_ref[...] = misc[:, V : V + 1] / (V * lat_total)


def finish(parts, points_total):
    return pl.pallas_call(
        functools.partial(finish_kernel, points_total),
        in_specs=[VMEM],
        out_shape=[
            jax.ShapeDtypeStruct((V, D), f32),
            jax.ShapeDtypeStruct((1, D), f32),
            jax.ShapeDtypeStruct((1, V), f32),
            jax.ShapeDtypeStruct((1, 1), f32),
        ],
        compiler_params=params(),
    )(parts)


def fields_kernel(points_total, fields_ref, grad_ref, weight_ref, gain_ref, lat_ref, out_ref):
    unit, inv_std = unit_of(fields_ref[...].astype(f32))
    slots = grad_ref.shape[0]
    grad = jnp.concatenate([grad_ref[k] for k in range(slots)], axis=1).astype(bf16)
    grad_normed = lax.dot_general(grad, weight_ref[...], TN, preferred_element_type=f32)
    grad_unit = grad_normed * gain_ref[...]
    mean_one = jnp.mean(grad_unit, axis=-1, keepdims=True)
    mean_two = jnp.mean(grad_unit * unit, axis=-1, keepdims=True)
    factor = points_total / lat_ref[0:1, 0:1]
    out_ref[...] = ((factor * inv_std) * (grad_unit - mean_one - unit * mean_two)).astype(bf16)


def fields_part(fields, grad, weight, gain, lat_total, points_total):
    slots = TILE // LANES
    return pl.pallas_call(
        functools.partial(fields_kernel, points_total),
        grid=(LOCAL // TILE,),
        in_specs=[
            pl.BlockSpec((TILE, D), lambda i: (i, 0)),
            pl.BlockSpec((slots, V, LANES), lambda i: (i, 0, 0)),
            pl.BlockSpec((V, D), lambda i: (0, 0)),
            pl.BlockSpec((1, D), lambda i: (0, 0)),
            pl.BlockSpec((8, LANES), lambda i: (0, 0)),
        ],
        out_specs=pl.BlockSpec((TILE, D), lambda i: (i, 0)),
        out_shape=jax.ShapeDtypeStruct((LOCAL, D), bf16),
        compiler_params=params(),
        cost_estimate=pl.CostEstimate(flops=2 * V * D * LOCAL, bytes_accessed=12 << 20, transcendentals=0),
    )(fields, grad, weight, gain, lat_total)


def swap(array, axes):
    return lax.all_to_all(array, axes, split_axis=0, concat_axis=0, tiled=True)


def shards(points_total, fields, observed, lat_weight, var_weight, weight, bias, gain):
    fields = fields.reshape(LOCAL, D)
    gain_row = gain.reshape(1, D)
    vw_row = var_weight.reshape(1, V)
    lat = lat_weight.reshape(M, LANES)
    slot = lax.axis_index(PLACE).astype(jnp.int32).reshape(1)
    core = lax.axis_index("core").astype(jnp.int32).reshape(1)
    pred, normed = forward(fields, weight, bias.reshape(1, V), gain_row)
    pred = swap(pred, PLACE)
    resid = residual(fields, gain_row)
    pred, resid = lax.optimization_barrier((pred, resid))
    grad, loss = pair(slot, pred, observed, lat, vw_row)
    grad = swap(grad, PLACE)
    sums = weight_part(grad, weight, gain_row, lat, loss, normed, resid)
    sums = lax.all_gather(sums, "core")
    sums = fold(core, sums)
    sums = swap(sums.reshape(CHIPS, 2, LANES), CHIP)
    sums, lat_total = share(sums.reshape(D // 2, LANES))
    sums = swap(sums.reshape(CHIPS, 2, LANES), CHIP)
    grad_fields = fields_part(fields, grad, weight, gain_row, lat_total, points_total)
    sums = lax.all_gather(sums.reshape(D // 2, LANES), "core", tiled=True)
    grad_weight, grad_gain, grad_bias, loss = finish(sums, points_total)
    return (
        grad_fields.reshape(1, LOCAL, D),
        grad_weight,
        grad_gain.reshape(D),
        grad_bias.reshape(V),
        loss.reshape(()),
    )


def solution(mesh):
    devices = mesh.devices.reshape(4, 2, 8, 4, 2)
    fine = Mesh(devices, ("x", "y_lo", "z", "y_hi", "core"))
    points_total = float(LOCAL * mesh.shape["grid"])
    return jax.shard_map(
        functools.partial(shards, points_total),
        mesh=fine,
        in_specs=(P(MEMBER, GRID, None), P(None, GRID), P(GRID), P(), P(), P(), P()),
        out_specs=(P(MEMBER, GRID, None), P(), P(), P(), P()),
        check_vma=False,
    )
```

```python
import functools
import jax
import jax.numpy as jnp
from jax import lax
from jax.experimental import pallas as pl
from jax.experimental.pallas import tpu as pltpu
from jax.sharding import Mesh, PartitionSpec as P

soft_square = 0.01
norm_epsilon = 1e-05

V = 100
M = 8
D = 1024
LOCAL = 1024
CHIPS = 256
LANES = 128
TILE = 256
BLOCK = 32
STEP = 512
ROWS = 104
GAIN_ROW, MISC_ROW, LAT_ROW = 100, 101, 102
GRID = ("x", "y_lo", "z")
MEMBER = ("y_hi", "core")
PLACE = ("core", "y_hi")
CHIP = ("x", "y_hi", "y_lo", "z")
VMEM_LIMIT = 16 * 1024 * 1024
FORWARD_VMEM = 60 * 1024 * 1024
RESIDUAL_VMEM = 60 * 1024 * 1024
WEIGHT_VMEM = 50 * 1024 * 1024
VMEM = pl.BlockSpec(memory_space=pltpu.VMEM)
SMEM = pl.BlockSpec(memory_space=pltpu.SMEM)
HBM = pl.BlockSpec(memory_space=pltpu.HBM)
f32, bf16, f8 = jnp.float32, jnp.bfloat16, jnp.float8_e4m3fn
RESIDUAL_SCALE = 512.0
NT = (((1,), (1,)), ((), ()))
TN = (((0,), (0,)), ((), ()))


def params(limit=VMEM_LIMIT):
    return pltpu.CompilerParams(vmem_limit_bytes=limit)


def column(row):
    n = row.shape[1]
    if n < LANES:
        row = jnp.concatenate([row, jnp.zeros((1, LANES - n), row.dtype)], axis=1)
    return jnp.broadcast_to(row, (LANES, LANES)).T


def unit_of(values):
    row_mean = jnp.mean(values, axis=-1, keepdims=True)
    centred = values - row_mean
    inv_std = lax.rsqrt(jnp.mean(centred * centred, axis=-1, keepdims=True) + norm_epsilon)
    return centred * inv_std, inv_std


def scaled_rows(fields_ref, rows, gain):
    unit, _ = unit_of(fields_ref[rows].astype(f32))
    return unit * gain


def forward_kernel(fields_hbm, weight_hbm, bias_hbm, gain_hbm, pred_hbm, normed_hbm,
                   fields_ref, weight_ref, bias_ref, gain_ref, pred_ref, normed_ref, in_sems, out_sems):
    tiles = LOCAL // TILE
    slots = TILE // LANES
    rows = [pl.ds(t * TILE, TILE) for t in range(tiles)]
    small = [
        pltpu.make_async_copy(gain_hbm, gain_ref, in_sems.at[tiles]),
        pltpu.make_async_copy(weight_hbm, weight_ref, in_sems.at[tiles + 1]),
        pltpu.make_async_copy(bias_hbm, bias_ref, in_sems.at[tiles + 2]),
    ]
    large = [
        pltpu.make_async_copy(fields_hbm.at[rows[t]], fields_ref.at[rows[t]], in_sems.at[t])
        for t in range(tiles)
    ]
    large[0].start()
    for copy in small:
        copy.start()
    for copy in large[1:]:
        copy.start()
    for copy in small:
        copy.wait()
    bias = column(bias_ref[...])[:V]
    back = []
    for t in range(tiles + 1):
        if t < tiles:
            large[t].wait()
            for start in range(t * TILE, (t + 1) * TILE, BLOCK):
                block = slice(start, start + BLOCK)
                normed_ref[block] = scaled_rows(fields_ref, block, gain_ref[...]).astype(bf16)
            back.append(pltpu.make_async_copy(normed_ref.at[rows[t]], normed_hbm.at[rows[t]], out_sems.at[t, 1]))
            back[-1].start()
        if t > 0:
            done = normed_ref[rows[t - 1]]
            pred = lax.dot_general(weight_ref[...], done, NT, preferred_element_type=f32)
            first = (t - 1) * slots
            for k in range(slots):
                pred_ref[first + k] = pred[:, k * LANES : (k + 1) * LANES] + bias
            here = pl.ds(first, slots)
            back.append(pltpu.make_async_copy(pred_ref.at[here], pred_hbm.at[here], out_sems.at[t - 1, 0]))
            back[-1].start()
    for copy in back:
        copy.wait()


def forward(fields, weight, bias, gain):
    tiles = LOCAL // TILE
    return pl.pallas_call(
        forward_kernel,
        in_specs=[HBM] * 4,
        out_specs=[HBM] * 2,
        out_shape=[
            jax.ShapeDtypeStruct((M, V, LANES), f32),
            jax.ShapeDtypeStruct((LOCAL, D), bf16),
        ],
        scratch_shapes=[
            pltpu.VMEM((LOCAL, D), bf16),
            pltpu.VMEM((V, D), bf16),
            pltpu.VMEM((1, V), f32),
            pltpu.VMEM((1, D), f32),
            pltpu.VMEM((M, V, LANES), f32),
            pltpu.VMEM((LOCAL, D), bf16),
            pltpu.SemaphoreType.DMA((tiles + 3,)),
            pltpu.SemaphoreType.DMA((tiles, 2)),
        ],
        compiler_params=params(FORWARD_VMEM),
        cost_estimate=pl.CostEstimate(flops=2 * V * D * LOCAL, bytes_accessed=3 << 20, transcendentals=0),
    )(fields, weight, bias, gain)


def residual_kernel(fields_ref, gain_ref, resid_ref):
    for start in range(0, TILE, BLOCK):
        block = slice(start, start + BLOCK)
        scaled = scaled_rows(fields_ref, block, gain_ref[...])
        rest = scaled - scaled.astype(bf16).astype(f32)
        resid_ref[block] = (rest * RESIDUAL_SCALE).astype(f8)


def residual(fields, gain):
    block = pl.BlockSpec((TILE, D), lambda i: (i, 0))
    return pl.pallas_call(
        residual_kernel,
        grid=(LOCAL // TILE,),
        in_specs=[block, pl.BlockSpec((1, D), lambda i: (0, 0))],
        out_specs=block,
        out_shape=jax.ShapeDtypeStruct((2 * LOCAL, D), f8),
        compiler_params=params(RESIDUAL_VMEM),
        cost_estimate=pl.CostEstimate(flops=12 * D * LOCAL, bytes_accessed=6 << 20, transcendentals=0),
    )(fields, gain)


def pair_kernel(slot_ref, pred_ref, obs_ref, lat_ref, vw_ref, grad_ref, loss_ref):
    here = pl.ds(pl.multiple_of(slot_ref[0] * LANES, LANES), LANES)
    vw = column(vw_ref[...])
    observed = obs_ref[:, here].astype(f32)
    lat = lat_ref[pl.ds(slot_ref[0], 1), :]
    loss = jnp.zeros((8, LANES), f32)
    for start in range(0, V, 8):
        rows = min(8, V - start)
        part = slice(start, start + rows)
        obs = observed[part]
        pred = [pred_ref[m, part] for m in range(M)]
        sign = [None] * M
        pair_abs = None
        obs_abs = None
        for m in range(M):
            gap = pred[m] - obs
            square = gap * gap + soft_square
            inverse = lax.rsqrt(square)
            size = square * inverse
            obs_abs = size if obs_abs is None else obs_abs + size
            sign[m] = gap * inverse * float(M - 1)
        for i in range(M):
            for j in range(i + 1, M):
                gap = pred[i] - pred[j]
                square = gap * gap + soft_square
                inverse = lax.rsqrt(square)
                size = square * inverse
                pair_abs = size if pair_abs is None else pair_abs + size
                term = gap * inverse
                sign[i] = sign[i] - term
                sign[j] = sign[j] + term
        scale = vw[part] * lat
        crps = obs_abs * (1.0 / M) - pair_abs * (1.0 / (M * (M - 1)))
        crps = crps * scale
        if rows < 8:
            crps = jnp.concatenate([crps, jnp.zeros((8 - rows, LANES), f32)], axis=0)
        loss = loss + crps
        scale = scale * (1.0 / (M * (M - 1)))
        for m in range(M):
            grad_ref[m, part] = sign[m] * scale
    loss_ref[...] = loss


def pair(slot, pred, observed, lat, var_weight):
    return pl.pallas_call(
        pair_kernel,
        in_specs=[SMEM] + [VMEM] * 4,
        out_specs=[VMEM] * 2,
        out_shape=[
            jax.ShapeDtypeStruct((M, V, LANES), f32),
            jax.ShapeDtypeStruct((8, LANES), f32),
        ],
        compiler_params=params(),
        cost_estimate=pl.CostEstimate(flops=1 << 20, bytes_accessed=1 << 19, transcendentals=0),
    )(slot, pred, observed, lat, var_weight)


def weight_kernel(grad_ref, weight_ref, gain_ref, lat_ref, loss_ref, normed_ref, resid_hbm, out_ref, resid_ref, sems):
    tiles = LOCAL // STEP
    copies = [
        pltpu.make_async_copy(
            resid_hbm.at[pl.ds(t * STEP, STEP)], resid_ref.at[pl.ds(t * STEP, STEP)], sems.at[t]
        )
        for t in range(tiles)
    ]
    for copy in copies:
        copy.start()
    grad = jnp.concatenate([grad_ref[k] for k in range(M)], axis=1).astype(bf16)
    ones = jnp.ones((8, LOCAL), bf16)
    sums = lax.dot_general(ones, grad, NT, preferred_element_type=f32)
    loss = jnp.sum(loss_ref[...], keepdims=True)
    lane = lax.broadcasted_iota(jnp.int32, (1, D), 1)
    misc = jnp.concatenate([sums[0:1], jnp.zeros((1, D - V), f32)], axis=1)
    misc = jnp.where(lane == V, loss, misc)
    lat = jnp.broadcast_to(jnp.sum(lat_ref[...], keepdims=True), (1, D))
    out_ref[:V] = jnp.dot(grad, normed_ref[...], preferred_element_type=f32)
    rest = jnp.zeros((V, D), f32)
    for t in range(tiles):
        copies[t].wait()
        rows = slice(t * STEP, (t + 1) * STEP)
        rest = rest + jnp.dot(grad[:, rows], resid_ref[rows].astype(bf16), preferred_element_type=f32)
    part_gain = weight_ref[...].astype(f32) * (out_ref[:V] + rest * (1.0 / RESIDUAL_SCALE))
    part_gain = jnp.sum(part_gain, axis=0, keepdims=True) / gain_ref[...]
    out_ref[V:] = jnp.concatenate([part_gain, misc, lat, jnp.zeros((1, D), f32)], axis=0)


def weight_part(grad, weight, gain, lat, loss, normed, resid):
    return pl.pallas_call(
        weight_kernel,
        in_specs=[VMEM] * 6 + [HBM],
        out_specs=VMEM,
        out_shape=jax.ShapeDtypeStruct((ROWS, D), f32),
        scratch_shapes=[
            pltpu.VMEM((LOCAL, D), f8),
            pltpu.SemaphoreType.DMA((LOCAL // STEP,)),
        ],
        compiler_params=params(WEIGHT_VMEM),
        cost_estimate=pl.CostEstimate(flops=4 * V * D * LOCAL, bytes_accessed=4 << 20, transcendentals=0),
    )(grad, weight, gain, lat, loss, normed, resid)


def fold_kernel(core_ref, parts_ref, out_ref):
    half = D // 2
    for k in range(half // LANES):
        start = pl.multiple_of(core_ref[0] * half + k * LANES, LANES)
        total = parts_ref[0, :, pl.ds(start, LANES)] + parts_ref[1, :, pl.ds(start, LANES)]
        total = jnp.concatenate([total, jnp.zeros((LANES - ROWS, LANES), f32)], axis=0)
        out_ref[k * LANES : (k + 1) * LANES] = total.T


def fold(core, parts):
    return pl.pallas_call(
        fold_kernel,
        in_specs=[SMEM, VMEM],
        out_specs=VMEM,
        out_shape=jax.ShapeDtypeStruct((D // 2, LANES), f32),
        compiler_params=params(),
    )(core, parts)


def share_kernel(parts_ref, out_ref, lat_ref):
    total = jnp.sum(parts_ref[...].reshape(D // 16, 8, LANES), axis=0)
    total = total + jnp.concatenate([total[4:], total[:4]], axis=0)
    total = total + jnp.concatenate([total[2:], total[:2]], axis=0)
    out_ref[...] = jnp.broadcast_to(total[None], (D // 16, 8, LANES)).reshape(D // 2, LANES)
    lat_ref[...] = jnp.broadcast_to(total[0:1, LAT_ROW : LAT_ROW + 1] * (1.0 / M), (8, LANES))


def share(parts):
    return pl.pallas_call(
        share_kernel,
        in_specs=[VMEM],
        out_specs=[VMEM, VMEM],
        out_shape=[
            jax.ShapeDtypeStruct((D // 2, LANES), f32),
            jax.ShapeDtypeStruct((8, LANES), f32),
        ],
        compiler_params=params(),
    )(parts)


def finish_kernel(points_total, parts_ref, weight_ref, gain_ref, bias_ref, loss_ref):
    lat_total = parts_ref[0:1, LAT_ROW : LAT_ROW + 1] * (1.0 / M)
    factor = points_total / lat_total
    for k in range(D // LANES):
        cols = slice(k * LANES, (k + 1) * LANES)
        block = parts_ref[cols].T
        weight_ref[:, cols] = block[:V] * factor
        gain_ref[:, cols] = block[GAIN_ROW : GAIN_ROW + 1] * factor
        if k == 0:
            misc = block[MISC_ROW : MISC_ROW + 1]
            bias_ref[...] = misc[:, :V] * factor
            loss_ref[...] = misc[:, V : V + 1] / (V * lat_total)


def finish(parts, points_total):
    return pl.pallas_call(
        functools.partial(finish_kernel, points_total),
        in_specs=[VMEM],
        out_shape=[
            jax.ShapeDtypeStruct((V, D), f32),
            jax.ShapeDtypeStruct((1, D), f32),
            jax.ShapeDtypeStruct((1, V), f32),
            jax.ShapeDtypeStruct((1, 1), f32),
        ],
        compiler_params=params(),
    )(parts)


def fields_kernel(points_total, fields_ref, grad_ref, weight_ref, gain_ref, lat_ref, out_ref):
    unit, inv_std = unit_of(fields_ref[...].astype(f32))
    slots = grad_ref.shape[0]
    grad = jnp.concatenate([grad_ref[k] for k in range(slots)], axis=1).astype(bf16)
    grad_normed = lax.dot_general(grad, weight_ref[...], TN, preferred_element_type=f32)
    grad_unit = grad_normed * gain_ref[...]
    mean_one = jnp.mean(grad_unit, axis=-1, keepdims=True)
    mean_two = jnp.mean(grad_unit * unit, axis=-1, keepdims=True)
    factor = points_total / lat_ref[0:1, 0:1]
    out_ref[...] = ((factor * inv_std) * (grad_unit - mean_one - unit * mean_two)).astype(bf16)


def fields_part(fields, grad, weight, gain, lat_total, points_total):
    slots = TILE // LANES
    return pl.pallas_call(
        functools.partial(fields_kernel, points_total),
        grid=(LOCAL // TILE,),
        in_specs=[
            pl.BlockSpec((TILE, D), lambda i: (i, 0)),
            pl.BlockSpec((slots, V, LANES), lambda i: (i, 0, 0)),
            pl.BlockSpec((V, D), lambda i: (0, 0)),
            pl.BlockSpec((1, D), lambda i: (0, 0)),
            pl.BlockSpec((8, LANES), lambda i: (0, 0)),
        ],
        out_specs=pl.BlockSpec((TILE, D), lambda i: (i, 0)),
        out_shape=jax.ShapeDtypeStruct((LOCAL, D), bf16),
        compiler_params=params(),
        cost_estimate=pl.CostEstimate(flops=2 * V * D * LOCAL, bytes_accessed=12 << 20, transcendentals=0),
    )(fields, grad, weight, gain, lat_total)


def swap(array, axes):
    return lax.all_to_all(array, axes, split_axis=0, concat_axis=0, tiled=True)


def shards(points_total, fields, observed, lat_weight, var_weight, weight, bias, gain):
    fields = fields.reshape(LOCAL, D)
    gain_row = gain.reshape(1, D)
    vw_row = var_weight.reshape(1, V)
    lat = lat_weight.reshape(M, LANES)
    slot = lax.axis_index(PLACE).astype(jnp.int32).reshape(1)
    core = lax.axis_index("core").astype(jnp.int32).reshape(1)
    pred, normed = forward(fields, weight, bias.reshape(1, V), gain_row)
    pred = swap(pred, PLACE)
    resid = residual(fields, gain_row)
    pred, resid = lax.optimization_barrier((pred, resid))
    grad, loss = pair(slot, pred, observed, lat, vw_row)
    grad = swap(grad, PLACE)
    sums = weight_part(grad, weight, gain_row, lat, loss, normed, resid)
    sums = lax.all_gather(sums, "core")
    sums = fold(core, sums)
    sums = swap(sums.reshape(CHIPS, 2, LANES), CHIP)
    sums, lat_total = share(sums.reshape(D // 2, LANES))
    sums = swap(sums.reshape(CHIPS, 2, LANES), CHIP)
    grad_fields = fields_part(fields, grad, weight, gain_row, lat_total, points_total)
    sums = lax.all_gather(sums.reshape(D // 2, LANES), "core", tiled=True)
    grad_weight, grad_gain, grad_bias, loss = finish(sums, points_total)
    return (
        grad_fields.reshape(1, LOCAL, D),
        grad_weight,
        grad_gain.reshape(D),
        grad_bias.reshape(V),
        loss.reshape(()),
    )


def solution(mesh):
    devices = mesh.devices.reshape(4, 2, 8, 4, 2)
    fine = Mesh(devices, ("x", "y_lo", "z", "y_hi", "core"))
    points_total = float(LOCAL * mesh.shape["grid"])
    return jax.shard_map(
        functools.partial(shards, points_total),
        mesh=fine,
        in_specs=(P(MEMBER, GRID, None), P(None, GRID), P(GRID), P(), P(), P(), P()),
        out_specs=(P(MEMBER, GRID, None), P(), P(), P(), P()),
        check_vma=False,
    )
```

```python
import functools
import jax
import jax.numpy as jnp
from jax import lax
from jax.experimental import pallas as pl
from jax.experimental.pallas import tpu as pltpu
from jax.sharding import Mesh, PartitionSpec as P

soft_square = 0.01
norm_epsilon = 1e-05

V = 100
M = 8
D = 1024
LOCAL = 1024
CHIPS = 256
LANES = 128
TILE = 256
BLOCK = 32
STEP = 512
ROWS = 104
GAIN_ROW, MISC_ROW, LAT_ROW = 100, 101, 102
GRID = ("x", "y_lo", "z")
MEMBER = ("y_hi", "core")
PLACE = ("core", "y_hi")
CHIP = ("x", "y_hi", "y_lo", "z")
VMEM_LIMIT = 16 * 1024 * 1024
FORWARD_VMEM = 60 * 1024 * 1024
RESIDUAL_VMEM = 60 * 1024 * 1024
WEIGHT_VMEM = 50 * 1024 * 1024
VMEM = pl.BlockSpec(memory_space=pltpu.VMEM)
SMEM = pl.BlockSpec(memory_space=pltpu.SMEM)
HBM = pl.BlockSpec(memory_space=pltpu.HBM)
f32, bf16, f8 = jnp.float32, jnp.bfloat16, jnp.float8_e4m3fn
RESIDUAL_SCALE = 512.0
NT = (((1,), (1,)), ((), ()))
TN = (((0,), (0,)), ((), ()))


def params(limit=VMEM_LIMIT):
    return pltpu.CompilerParams(vmem_limit_bytes=limit)


def column(row):
    n = row.shape[1]
    if n < LANES:
        row = jnp.concatenate([row, jnp.zeros((1, LANES - n), row.dtype)], axis=1)
    return jnp.broadcast_to(row, (LANES, LANES)).T


def unit_of(values):
    row_mean = jnp.mean(values, axis=-1, keepdims=True)
    centred = values - row_mean
    inv_std = lax.rsqrt(jnp.mean(centred * centred, axis=-1, keepdims=True) + norm_epsilon)
    return centred * inv_std, inv_std


def scaled_rows(fields_ref, rows, gain):
    unit, _ = unit_of(fields_ref[rows].astype(f32))
    return unit * gain


def forward_kernel(fields_hbm, weight_hbm, bias_hbm, gain_hbm, pred_hbm, normed_hbm,
                   fields_ref, weight_ref, bias_ref, gain_ref, pred_ref, normed_ref, in_sems, out_sems):
    tiles = LOCAL // TILE
    slots = TILE // LANES
    rows = [pl.ds(t * TILE, TILE) for t in range(tiles)]
    small = [
        pltpu.make_async_copy(gain_hbm, gain_ref, in_sems.at[tiles]),
        pltpu.make_async_copy(weight_hbm, weight_ref, in_sems.at[tiles + 1]),
        pltpu.make_async_copy(bias_hbm, bias_ref, in_sems.at[tiles + 2]),
    ]
    large = [
        pltpu.make_async_copy(fields_hbm.at[rows[t]], fields_ref.at[rows[t]], in_sems.at[t])
        for t in range(tiles)
    ]
    large[0].start()
    for copy in small:
        copy.start()
    for copy in large[1:]:
        copy.start()
    small[0].wait()
    back = []
    for t in range(tiles + 1):
        if t < tiles:
            large[t].wait()
            for start in range(t * TILE, (t + 1) * TILE, BLOCK):
                block = slice(start, start + BLOCK)
                normed_ref[block] = scaled_rows(fields_ref, block, gain_ref[...]).astype(bf16)
            back.append(pltpu.make_async_copy(normed_ref.at[rows[t]], normed_hbm.at[rows[t]], out_sems.at[t, 1]))
            back[-1].start()
        if t == 1:
            for copy in small[1:]:
                copy.wait()
            bias = column(bias_ref[...])[:V]
        if t > 0:
            done = normed_ref[rows[t - 1]]
            pred = lax.dot_general(weight_ref[...], done, NT, preferred_element_type=f32)
            first = (t - 1) * slots
            for k in range(slots):
                pred_ref[first + k] = pred[:, k * LANES : (k + 1) * LANES] + bias
            here = pl.ds(first, slots)
            back.append(pltpu.make_async_copy(pred_ref.at[here], pred_hbm.at[here], out_sems.at[t - 1, 0]))
            back[-1].start()
    for copy in back:
        copy.wait()


def forward(fields, weight, bias, gain):
    tiles = LOCAL // TILE
    return pl.pallas_call(
        forward_kernel,
        in_specs=[HBM] * 4,
        out_specs=[HBM] * 2,
        out_shape=[
            jax.ShapeDtypeStruct((M, V, LANES), f32),
            jax.ShapeDtypeStruct((LOCAL, D), bf16),
        ],
        scratch_shapes=[
            pltpu.VMEM((LOCAL, D), bf16),
            pltpu.VMEM((V, D), bf16),
            pltpu.VMEM((1, V), f32),
            pltpu.VMEM((1, D), f32),
            pltpu.VMEM((M, V, LANES), f32),
            pltpu.VMEM((LOCAL, D), bf16),
            pltpu.SemaphoreType.DMA((tiles + 3,)),
            pltpu.SemaphoreType.DMA((tiles, 2)),
        ],
        compiler_params=params(FORWARD_VMEM),
        cost_estimate=pl.CostEstimate(flops=2 * V * D * LOCAL, bytes_accessed=3 << 20, transcendentals=0),
    )(fields, weight, bias, gain)


def residual_kernel(fields_ref, gain_ref, resid_ref):
    for start in range(0, TILE, BLOCK):
        block = slice(start, start + BLOCK)
        scaled = scaled_rows(fields_ref, block, gain_ref[...])
        rest = scaled - scaled.astype(bf16).astype(f32)
        resid_ref[block] = (rest * RESIDUAL_SCALE).astype(f8)


def residual(fields, gain):
    block = pl.BlockSpec((TILE, D), lambda i: (i, 0))
    return pl.pallas_call(
        residual_kernel,
        grid=(LOCAL // TILE,),
        in_specs=[block, pl.BlockSpec((1, D), lambda i: (0, 0))],
        out_specs=block,
        out_shape=jax.ShapeDtypeStruct((2 * LOCAL, D), f8),
        compiler_params=params(RESIDUAL_VMEM),
        cost_estimate=pl.CostEstimate(flops=12 * D * LOCAL, bytes_accessed=6 << 20, transcendentals=0),
    )(fields, gain)


def pair_kernel(slot_ref, pred_ref, obs_ref, lat_ref, vw_ref, grad_ref, loss_ref):
    here = pl.ds(pl.multiple_of(slot_ref[0] * LANES, LANES), LANES)
    vw = column(vw_ref[...])
    observed = obs_ref[:, here].astype(f32)
    lat = lat_ref[pl.ds(slot_ref[0], 1), :]
    loss = jnp.zeros((8, LANES), f32)
    for start in range(0, V, 8):
        rows = min(8, V - start)
        part = slice(start, start + rows)
        obs = observed[part]
        pred = [pred_ref[m, part] for m in range(M)]
        sign = [None] * M
        pair_abs = None
        obs_abs = None
        for m in range(M):
            gap = pred[m] - obs
            square = gap * gap + soft_square
            inverse = lax.rsqrt(square)
            size = square * inverse
            obs_abs = size if obs_abs is None else obs_abs + size
            sign[m] = gap * inverse * float(M - 1)
        for i in range(M):
            for j in range(i + 1, M):
                gap = pred[i] - pred[j]
                square = gap * gap + soft_square
                inverse = lax.rsqrt(square)
                size = square * inverse
                pair_abs = size if pair_abs is None else pair_abs + size
                term = gap * inverse
                sign[i] = sign[i] - term
                sign[j] = sign[j] + term
        scale = vw[part] * lat
        crps = obs_abs * (1.0 / M) - pair_abs * (1.0 / (M * (M - 1)))
        crps = crps * scale
        if rows < 8:
            crps = jnp.concatenate([crps, jnp.zeros((8 - rows, LANES), f32)], axis=0)
        loss = loss + crps
        scale = scale * (1.0 / (M * (M - 1)))
        for m in range(M):
            grad_ref[m, part] = sign[m] * scale
    loss_ref[...] = loss


def pair(slot, pred, observed, lat, var_weight):
    return pl.pallas_call(
        pair_kernel,
        in_specs=[SMEM] + [VMEM] * 4,
        out_specs=[VMEM] * 2,
        out_shape=[
            jax.ShapeDtypeStruct((M, V, LANES), f32),
            jax.ShapeDtypeStruct((8, LANES), f32),
        ],
        compiler_params=params(),
        cost_estimate=pl.CostEstimate(flops=1 << 20, bytes_accessed=1 << 19, transcendentals=0),
    )(slot, pred, observed, lat, var_weight)


def weight_kernel(grad_ref, weight_ref, gain_ref, lat_ref, loss_ref, normed_ref, resid_hbm, out_ref, resid_ref, sems):
    tiles = LOCAL // STEP
    copies = [
        pltpu.make_async_copy(
            resid_hbm.at[pl.ds(t * STEP, STEP)], resid_ref.at[pl.ds(t * STEP, STEP)], sems.at[t]
        )
        for t in range(tiles)
    ]
    for copy in copies:
        copy.start()
    grad = jnp.concatenate([grad_ref[k] for k in range(M)], axis=1).astype(bf16)
    ones = jnp.ones((8, LOCAL), bf16)
    sums = lax.dot_general(ones, grad, NT, preferred_element_type=f32)
    loss = jnp.sum(loss_ref[...], keepdims=True)
    lane = lax.broadcasted_iota(jnp.int32, (1, D), 1)
    misc = jnp.concatenate([sums[0:1], jnp.zeros((1, D - V), f32)], axis=1)
    misc = jnp.where(lane == V, loss, misc)
    lat = jnp.broadcast_to(jnp.sum(lat_ref[...], keepdims=True), (1, D))
    out_ref[:V] = jnp.dot(grad, normed_ref[...], preferred_element_type=f32)
    rest = jnp.zeros((V, D), f32)
    for t in range(tiles):
        copies[t].wait()
        rows = slice(t * STEP, (t + 1) * STEP)
        rest = rest + jnp.dot(grad[:, rows], resid_ref[rows].astype(bf16), preferred_element_type=f32)
    part_gain = weight_ref[...].astype(f32) * (out_ref[:V] + rest * (1.0 / RESIDUAL_SCALE))
    part_gain = jnp.sum(part_gain, axis=0, keepdims=True) / gain_ref[...]
    out_ref[V:] = jnp.concatenate([part_gain, misc, lat, jnp.zeros((1, D), f32)], axis=0)


def weight_part(grad, weight, gain, lat, loss, normed, resid):
    return pl.pallas_call(
        weight_kernel,
        in_specs=[VMEM] * 6 + [HBM],
        out_specs=VMEM,
        out_shape=jax.ShapeDtypeStruct((ROWS, D), f32),
        scratch_shapes=[
            pltpu.VMEM((LOCAL, D), f8),
            pltpu.SemaphoreType.DMA((LOCAL // STEP,)),
        ],
        compiler_params=params(WEIGHT_VMEM),
        cost_estimate=pl.CostEstimate(flops=4 * V * D * LOCAL, bytes_accessed=4 << 20, transcendentals=0),
    )(grad, weight, gain, lat, loss, normed, resid)


def fold_kernel(core_ref, parts_ref, out_ref):
    half = D // 2
    for k in range(half // LANES):
        start = pl.multiple_of(core_ref[0] * half + k * LANES, LANES)
        total = parts_ref[0, :, pl.ds(start, LANES)] + parts_ref[1, :, pl.ds(start, LANES)]
        total = jnp.concatenate([total, jnp.zeros((LANES - ROWS, LANES), f32)], axis=0)
        out_ref[k * LANES : (k + 1) * LANES] = total.T


def fold(core, parts):
    return pl.pallas_call(
        fold_kernel,
        in_specs=[SMEM, VMEM],
        out_specs=VMEM,
        out_shape=jax.ShapeDtypeStruct((D // 2, LANES), f32),
        compiler_params=params(),
    )(core, parts)


def share_kernel(parts_ref, out_ref, lat_ref):
    total = jnp.sum(parts_ref[...].reshape(D // 16, 8, LANES), axis=0)
    total = total + jnp.concatenate([total[4:], total[:4]], axis=0)
    total = total + jnp.concatenate([total[2:], total[:2]], axis=0)
    out_ref[...] = jnp.broadcast_to(total[None], (D // 16, 8, LANES)).reshape(D // 2, LANES)
    lat_ref[...] = jnp.broadcast_to(total[0:1, LAT_ROW : LAT_ROW + 1] * (1.0 / M), (8, LANES))


def share(parts):
    return pl.pallas_call(
        share_kernel,
        in_specs=[VMEM],
        out_specs=[VMEM, VMEM],
        out_shape=[
            jax.ShapeDtypeStruct((D // 2, LANES), f32),
            jax.ShapeDtypeStruct((8, LANES), f32),
        ],
        compiler_params=params(),
    )(parts)


def finish_kernel(points_total, parts_ref, weight_ref, gain_ref, bias_ref, loss_ref):
    lat_total = parts_ref[0:1, LAT_ROW : LAT_ROW + 1] * (1.0 / M)
    factor = points_total / lat_total
    for k in range(D // LANES):
        cols = slice(k * LANES, (k + 1) * LANES)
        block = parts_ref[cols].T
        weight_ref[:, cols] = block[:V] * factor
        gain_ref[:, cols] = block[GAIN_ROW : GAIN_ROW + 1] * factor
        if k == 0:
            misc = block[MISC_ROW : MISC_ROW + 1]
            bias_ref[...] = misc[:, :V] * factor
            loss_ref[...] = misc[:, V : V + 1] / (V * lat_total)


def finish(parts, points_total):
    return pl.pallas_call(
        functools.partial(finish_kernel, points_total),
        in_specs=[VMEM],
        out_shape=[
            jax.ShapeDtypeStruct((V, D), f32),
            jax.ShapeDtypeStruct((1, D), f32),
            jax.ShapeDtypeStruct((1, V), f32),
            jax.ShapeDtypeStruct((1, 1), f32),
        ],
        compiler_params=params(),
    )(parts)


def fields_kernel(points_total, fields_ref, grad_ref, weight_ref, gain_ref, lat_ref, out_ref):
    unit, inv_std = unit_of(fields_ref[...].astype(f32))
    slots = grad_ref.shape[0]
    grad = jnp.concatenate([grad_ref[k] for k in range(slots)], axis=1).astype(bf16)
    grad_normed = lax.dot_general(grad, weight_ref[...], TN, preferred_element_type=f32)
    grad_unit = grad_normed * gain_ref[...]
    mean_one = jnp.mean(grad_unit, axis=-1, keepdims=True)
    mean_two = jnp.mean(grad_unit * unit, axis=-1, keepdims=True)
    factor = points_total / lat_ref[0:1, 0:1]
    out_ref[...] = ((factor * inv_std) * (grad_unit - mean_one - unit * mean_two)).astype(bf16)


def fields_part(fields, grad, weight, gain, lat_total, points_total):
    slots = TILE // LANES
    return pl.pallas_call(
        functools.partial(fields_kernel, points_total),
        grid=(LOCAL // TILE,),
        in_specs=[
            pl.BlockSpec((TILE, D), lambda i: (i, 0)),
            pl.BlockSpec((slots, V, LANES), lambda i: (i, 0, 0)),
            pl.BlockSpec((V, D), lambda i: (0, 0)),
            pl.BlockSpec((1, D), lambda i: (0, 0)),
            pl.BlockSpec((8, LANES), lambda i: (0, 0)),
        ],
        out_specs=pl.BlockSpec((TILE, D), lambda i: (i, 0)),
        out_shape=jax.ShapeDtypeStruct((LOCAL, D), bf16),
        compiler_params=params(),
        cost_estimate=pl.CostEstimate(flops=2 * V * D * LOCAL, bytes_accessed=12 << 20, transcendentals=0),
    )(fields, grad, weight, gain, lat_total)


def swap(array, axes):
    return lax.all_to_all(array, axes, split_axis=0, concat_axis=0, tiled=True)


def shards(points_total, fields, observed, lat_weight, var_weight, weight, bias, gain):
    fields = fields.reshape(LOCAL, D)
    gain_row = gain.reshape(1, D)
    vw_row = var_weight.reshape(1, V)
    lat = lat_weight.reshape(M, LANES)
    slot = lax.axis_index(PLACE).astype(jnp.int32).reshape(1)
    core = lax.axis_index("core").astype(jnp.int32).reshape(1)
    pred, normed = forward(fields, weight, bias.reshape(1, V), gain_row)
    pred = swap(pred, PLACE)
    resid = residual(fields, gain_row)
    pred, resid = lax.optimization_barrier((pred, resid))
    grad, loss = pair(slot, pred, observed, lat, vw_row)
    grad = swap(grad, PLACE)
    sums = weight_part(grad, weight, gain_row, lat, loss, normed, resid)
    sums = lax.all_gather(sums, "core")
    sums = fold(core, sums)
    sums = swap(sums.reshape(CHIPS, 2, LANES), CHIP)
    sums, lat_total = share(sums.reshape(D // 2, LANES))
    sums = swap(sums.reshape(CHIPS, 2, LANES), CHIP)
    grad_fields = fields_part(fields, grad, weight, gain_row, lat_total, points_total)
    sums = lax.all_gather(sums.reshape(D // 2, LANES), "core", tiled=True)
    grad_weight, grad_gain, grad_bias, loss = finish(sums, points_total)
    return (
        grad_fields.reshape(1, LOCAL, D),
        grad_weight,
        grad_gain.reshape(D),
        grad_bias.reshape(V),
        loss.reshape(()),
    )


def solution(mesh):
    devices = mesh.devices.reshape(4, 2, 8, 4, 2)
    fine = Mesh(devices, ("x", "y_lo", "z", "y_hi", "core"))
    points_total = float(LOCAL * mesh.shape["grid"])
    return jax.shard_map(
        functools.partial(shards, points_total),
        mesh=fine,
        in_specs=(P(MEMBER, GRID, None), P(None, GRID), P(GRID), P(), P(), P(), P()),
        out_specs=(P(MEMBER, GRID, None), P(), P(), P(), P()),
        check_vma=False,
    )
```
